32 devices in a mesh: bev: 8 (over z, x), scene: 4 (over y, core).
Axes of the slice: x: 2, y: 2, z: 4, core: 2. Of those that a mesh axis runs over, the one named last changes fastest.
Arguments:
- context: bfloat16 [4, 80, 2048], P('scene', None, 'bev'), may hold values from -24 to 24
- depth_logits: float32 [4, 112, 2048], P('scene', None, 'bev'), may hold values from -20 to 300
- send_count: int32 [4, 8, 8], P('scene', 'bev'), may hold values from 0 to 1024, as said below
- slot_point: int32 [4, 8, 8, 1024], P('scene', 'bev'), may hold values from 0 to 28671, as said below
- slot_cell: int32 [4, 8, 8, 1024], P('scene', 'bev'), may hold values from 0 to 2047
Outputs:
- bev_features: bfloat16 [16384, 320], P(('bev', 'scene'))
The draws below stay inside these ranges and needn't reach their ends.
Inputs may be any that keep to these rules, and one draw needn't show every extreme that they name: `send_count`: one entry is 1024 in every pixel block's row. `slot_point`: the live slots of one pixel block name distinct points; slots at or past the count are unused.
All inputs are finite; a program needn't handle non-finite values.
Results may differ from the reference program's by a relative error of at most 0.0062.
Values may be sent and summed in bfloat16 or wider, within the bound.
A program may use at most 128 MiB of HBM per device.

```python
import jax
import jax.numpy as jnp
from jax import lax

C = 80
DEPTH = 112
GRID = 128
PIX_DEV = 256
STRIPS = 8
SCENES = 4
PIXELS = 2048
CAP = 1024


def draw_context(key, part):
    keys = jax.random.split(jax.random.fold_in(key, 5), 3)
    values = 4.0 * jax.random.normal(keys[2], (SCENES, C, PIXELS), jnp.float32)
    return jnp.clip(values, -24.0, 24.0).astype(jnp.bfloat16)


def draw_depth_logits(key, part):
    keys = jax.random.split(jax.random.fold_in(key, 11), 10)
    base = 0.5 * jax.random.normal(keys[9], (SCENES, DEPTH, PIXELS), jnp.float32)
    return jnp.clip(base, -3.0, 3.0).astype(jnp.float32)


def routing_tables(key):
    base_key = jax.random.fold_in(key, 7)
    strip_cells = GRID * GRID // STRIPS
    point_total = PIX_DEV * DEPTH

    def one_block(sub):
        keys = jax.random.split(sub, 6)
        window_start = jax.random.randint(keys[0], (), 0, STRIPS)
        strip_ids = jnp.arange(STRIPS, dtype=jnp.int32)
        inside = (strip_ids - window_start) % STRIPS < STRIPS // 4
        heavy = jax.random.randint(keys[1], (STRIPS,), 3 * CAP // 4, CAP + 1)
        light = jax.random.randint(keys[2], (STRIPS,), 0, CAP // 6 + 1)
        counts = jnp.where(inside, heavy, light)
        full_strip = (window_start + jax.random.randint(keys[3], (), 0, STRIPS // 4)) % STRIPS
        counts = jnp.where(strip_ids == full_strip, CAP, counts).astype(jnp.int32)
        order = jax.random.permutation(keys[4], point_total).astype(jnp.int32)
        offset = jnp.cumsum(counts) - counts
        positions = (offset[:, None] + jnp.arange(CAP, dtype=jnp.int32)[None, :]) % point_total
        points = order[positions]
        cells = jax.random.randint(keys[5], (STRIPS, CAP), 0, strip_cells)
        return (counts, points, cells)
    subkeys = jax.random.split(base_key, SCENES * STRIPS)
    counts, points, cells = jax.vmap(one_block)(subkeys)
    return (counts.reshape(SCENES, STRIPS, STRIPS), points.reshape(SCENES, STRIPS, STRIPS, CAP), cells.reshape(SCENES, STRIPS, STRIPS, CAP))


def draw_send_count(key, part):
    return routing_tables(key)[0].astype(jnp.int32)


def draw_slot_point(key, part):
    return routing_tables(key)[1].astype(jnp.int32)


def draw_slot_cell(key, part):
    return routing_tables(key)[2].astype(jnp.int32)


def setup_inputs(seed: int = 0) -> dict:
    streams_of = jax.random.split(jax.random.key(seed), 6)
    return {
        "context": draw_context(jax.random.fold_in(streams_of[5], 71), 0),
        "depth_logits": draw_depth_logits(jax.random.fold_in(streams_of[5], 71), 0),
        "send_count": draw_send_count(jax.random.fold_in(streams_of[5], 71), 0),
        "slot_point": draw_slot_point(jax.random.fold_in(streams_of[5], 71), 0),
        "slot_cell": draw_slot_cell(jax.random.fold_in(streams_of[5], 71), 0),
    }


def reference(context, depth_logits, send_count, slot_point, slot_cell):
    depth_prob = jax.nn.softmax(depth_logits.astype(jnp.float32), axis=1).astype(jnp.bfloat16)
    strip_cells = GRID * GRID // STRIPS

    def scene_sum(blocks):
        scene_ctx, scene_prob, scene_count, scene_points, scene_cells = blocks

        def add_source(running, source):
            ctx_block = lax.dynamic_slice_in_dim(scene_ctx, source * PIX_DEV, PIX_DEV, 1)
            prob_block = lax.dynamic_slice_in_dim(scene_prob, source * PIX_DEV, PIX_DEV, 1)
            point_ids = scene_points[source].reshape(-1)
            depth_bin = point_ids // PIX_DEV
            pixel_ids = point_ids % PIX_DEV
            weight = prob_block[depth_bin, pixel_ids].astype(jnp.float32)
            features = ctx_block[:, pixel_ids].T.astype(jnp.float32)
            values = (features * weight[:, None]).astype(jnp.bfloat16)
            live_mask = jnp.arange(CAP, dtype=jnp.int32)[None, :] < scene_count[source][:, None]
            strip_base = jnp.arange(STRIPS, dtype=jnp.int32)[:, None] * strip_cells
            targets = jnp.where(live_mask, strip_base + scene_cells[source], GRID * GRID).reshape(-1).astype(jnp.int32)
            pooled = jax.ops.segment_sum(values.astype(jnp.float32), targets, num_segments=GRID * GRID + 1)
            return running + pooled[:GRID * GRID], None

        running, _ = lax.scan(add_source, jnp.zeros((GRID * GRID, C), jnp.float32), jnp.arange(STRIPS, dtype=jnp.int32))
        return running

    sums = lax.map(scene_sum, (context, depth_prob, send_count, slot_point, slot_cell))
    return jnp.transpose(sums, (1, 0, 2)).reshape(GRID * GRID, SCENES * C).astype(jnp.bfloat16)
```

```python
import functools

import jax
import jax.numpy as jnp
from jax import lax
from jax.experimental import pallas as pl
from jax.experimental.pallas import tpu as pltpu
from jax.sharding import PartitionSpec as P

GRID = 128
LANES = 128
LOW = 4
MESH = pl.DeviceIdType.MESH


def kernel(strips, scenes, strip_cells, context_ref, logits_ref, count_ref, point_ref, cell_ref,
           out_ref, context_all, sent, got, prob, total, parts,
           ctx_send, ctx_recv, slot_send, slot_recv, part_send, part_recv):
    channels, pix_block = context_ref.shape
    depth_bins = logits_ref.shape[0]
    capacity = point_ref.shape[1]
    rows = capacity // LANES
    quarter = strip_cells // scenes
    sub = quarter // LOW
    me = lax.axis_index("bev")
    scene = lax.axis_index("scene")

    barrier = pltpu.get_barrier_semaphore()

    @pl.loop(1, strips)
    def _(step):
        pl.semaphore_signal(barrier, inc=1, device_id={"bev": lax.rem(me + step, strips)}, device_id_type=MESH)

    @pl.loop(1, scenes)
    def _(step):
        pl.semaphore_signal(barrier, inc=1, device_id={"scene": lax.rem(scene + step, scenes)}, device_id_type=MESH)

    logits = logits_ref[...]
    powers = jnp.exp(logits - jnp.max(logits, axis=0, keepdims=True))
    prob[...] = (powers / jnp.sum(powers, axis=0, keepdims=True)).astype(jnp.bfloat16)
    pl.semaphore_wait(barrier, strips - 1 + scenes - 1)

    def context_copy(step):
        return pltpu.make_async_remote_copy(
            src_ref=context_ref, dst_ref=context_all.at[me],
            send_sem=ctx_send.at[step], recv_sem=ctx_recv.at[me],
            device_id={"bev": lax.rem(me + step, strips)}, device_id_type=MESH)

    def slot_copy(step):
        to = lax.rem(me + step, strips)
        return pltpu.make_async_remote_copy(
            src_ref=sent.at[to], dst_ref=got.at[me],
            send_sem=slot_send.at[step], recv_sem=slot_recv.at[me],
            device_id={"bev": to}, device_id_type=MESH)

    @pl.loop(1, strips)
    def _(step):
        context_copy(step).start()

    pixel_row = lax.broadcasted_iota(jnp.int32, (pix_block, capacity), 0)
    depth_row = lax.broadcasted_iota(jnp.int32, (depth_bins, capacity), 0)
    slot_row = lax.broadcasted_iota(jnp.int32, (1, capacity), 1)

    def fill(to):
        points = point_ref[pl.ds(to, 1), :]
        live = slot_row < count_ref[0, to]
        pixel = points % pix_block
        depth = points // pix_block
        hot = jnp.where(pixel_row == pixel, 1.0, 0.0).astype(jnp.bfloat16)
        column = jnp.dot(prob[...], hot, preferred_element_type=jnp.float32)
        weight = jnp.sum(jnp.where(depth_row == depth, column, 0.0), axis=0, keepdims=True)
        weight = jnp.where(live, weight, 0.0)
        cell = jnp.where(live, cell_ref[pl.ds(to, 1), :], strip_cells)
        code = (cell * pix_block + pixel).astype(jnp.float32)
        for r in range(rows):
            sent[to, r:r + 1, :] = weight[:, r * LANES:(r + 1) * LANES]
            sent[to, rows + r:rows + r + 1, :] = code[:, r * LANES:(r + 1) * LANES]

    @pl.loop(1, strips)
    def _(step):
        fill(lax.rem(me + step, strips))
        slot_copy(step).start()

    fill(me)
    total[...] = jnp.zeros_like(total)
    high_row = lax.broadcasted_iota(jnp.int32, (scenes * sub, capacity), 0)

    def pool(features_map, slots):
        weight = jnp.concatenate([slots[r:r + 1, :] for r in range(rows)], axis=1)
        code = jnp.concatenate([slots[rows + r:rows + r + 1, :] for r in range(rows)], axis=1).astype(jnp.int32)
        pixel = code % pix_block
        cell = code // pix_block
        high = (cell // quarter) * sub + cell % sub
        low = (cell // sub) % LOW
        pixel_hot = jnp.where(pixel_row == pixel, 1.0, 0.0).astype(jnp.bfloat16)
        features = jnp.dot(features_map, pixel_hot, preferred_element_type=jnp.float32)
        values = features * weight
        spread = jnp.concatenate(
            [jnp.where(low == j, values, 0.0).astype(jnp.bfloat16) for j in range(LOW)], axis=0)
        high_hot = jnp.where(high_row == high, 1.0, 0.0).astype(jnp.bfloat16)
        total[...] += lax.dot_general(
            spread, high_hot, (((1,), (1,)), ((), ())), preferred_element_type=jnp.float32)

    pool(context_ref[...], sent[me])

    @pl.loop(1, strips)
    def _(step):
        source = lax.rem(me + strips - step, strips)
        pltpu.make_async_remote_copy(
            src_ref=context_ref, dst_ref=context_all.at[source],
            send_sem=ctx_send.at[step], recv_sem=ctx_recv.at[source],
            device_id={"bev": source}, device_id_type=MESH).wait_recv()
        pltpu.make_async_remote_copy(
            src_ref=sent.at[source], dst_ref=got.at[source],
            send_sem=slot_send.at[step], recv_sem=slot_recv.at[source],
            device_id={"bev": source}, device_id_type=MESH).wait_recv()
        pool(context_all[source], got[source])

    for q in range(scenes):
        for j in range(LOW):
            parts[q, j] = total[j * channels:(j + 1) * channels, q * sub:(q + 1) * sub].astype(jnp.bfloat16)

    def part_copy(step):
        to = lax.rem(scene + step, scenes)
        return pltpu.make_async_remote_copy(
            src_ref=parts.at[to], dst_ref=out_ref.at[:, pl.ds(pl.multiple_of(scene * channels, 16), channels), :],
            send_sem=part_send.at[step], recv_sem=part_recv.at[scene],
            device_id={"scene": to}, device_id_type=MESH)

    @pl.loop(1, scenes)
    def _(step):
        part_copy(step).start()

    out_ref[:, pl.ds(pl.multiple_of(scene * channels, 16), channels), :] = parts[scene]

    @pl.loop(1, strips)
    def _(step):
        context_copy(step).wait_send()
        slot_copy(step).wait_send()

    @pl.loop(1, scenes)
    def _(step):
        source = lax.rem(scene + scenes - step, scenes)
        pltpu.make_async_remote_copy(
            src_ref=parts.at[source],
            dst_ref=out_ref.at[:, pl.ds(pl.multiple_of(source * channels, 16), channels), :],
            send_sem=part_send.at[step], recv_sem=part_recv.at[source],
            device_id={"scene": source}, device_id_type=MESH).wait_recv()
        part_copy(step).wait_send()


def body(context, depth_logits, send_count, slot_point, slot_cell):
    strips = lax.axis_size("bev")
    scenes = lax.axis_size("scene")
    strip_cells = GRID * GRID // strips
    channels, pix_block = context.shape[1:]
    depth_bins = depth_logits.shape[1]
    capacity = slot_point.shape[3]
    quarter = strip_cells // scenes
    sub = quarter // LOW
    vmem = pl.BlockSpec(memory_space=pltpu.VMEM)
    slots = (strips, 2 * capacity // LANES, LANES)
    pooled = pl.pallas_call(
        functools.partial(kernel, strips, scenes, strip_cells),
        out_shape=jax.ShapeDtypeStruct((LOW, scenes * channels, sub), jnp.bfloat16),
        in_specs=[vmem, vmem, pl.BlockSpec(memory_space=pltpu.SMEM), vmem, vmem],
        out_specs=vmem,
        scratch_shapes=[
            pltpu.VMEM((strips, channels, pix_block), jnp.bfloat16),
            pltpu.VMEM(slots, jnp.float32),
            pltpu.VMEM(slots, jnp.float32),
            pltpu.VMEM((depth_bins, pix_block), jnp.bfloat16),
            pltpu.VMEM((LOW * channels, scenes * sub), jnp.float32),
            pltpu.VMEM((scenes, LOW, channels, sub), jnp.bfloat16),
            pltpu.SemaphoreType.DMA((strips,)),
            pltpu.SemaphoreType.DMA((strips,)),
            pltpu.SemaphoreType.DMA((strips,)),
            pltpu.SemaphoreType.DMA((strips,)),
            pltpu.SemaphoreType.DMA((scenes,)),
            pltpu.SemaphoreType.DMA((scenes,)),
        ],
        compiler_params=pltpu.CompilerParams(
            collective_id=0, has_side_effects=True, vmem_limit_bytes=48 * 1024 * 1024),
    )(context[0], depth_logits[0], send_count[0], slot_point[0, 0], slot_cell[0, 0])
    return jnp.transpose(pooled, (0, 2, 1)).reshape(quarter, scenes * channels)


def solution(mesh):
    return jax.shard_map(
        body,
        mesh=mesh,
        in_specs=(
            P("scene", None, "bev"),
            P("scene", None, "bev"),
            P("scene", "bev", None),
            P("scene", "bev", None, None),
            P("scene", "bev", None, None),
        ),
        out_specs=P(("bev", "scene"), None),
        check_vma=False,
    )
```

```python
import functools

import jax
import jax.numpy as jnp
from jax import lax
from jax.experimental import pallas as pl
from jax.experimental.pallas import tpu as pltpu
from jax.sharding import PartitionSpec as P

GRID = 128
LANES = 128
LOW = 4
HALVES = 2
MESH = pl.DeviceIdType.MESH


def kernel(strips, scenes, strip_cells, context_hbm, logits_hbm, count_hbm, point_hbm, cell_hbm,
           out_ref, context_ref, logits_ref, count_ref, point_ref, cell_ref,
           context_all, sent, got, prob, values_all, total, parts,
           load, ctx_send, ctx_recv, slot_send, slot_recv, part_send, part_recv):
    channels, pix_block = context_ref.shape
    depth_bins = logits_ref.shape[0]
    capacity = point_ref.shape[1]
    rows = capacity // LANES
    quarter = strip_cells // scenes
    sub = quarter // LOW
    group = scenes // HALVES
    half_rows = group * sub
    assert pix_block <= 256 and half_rows <= 256
    me = lax.axis_index("bev")
    scene = lax.axis_index("scene")

    loads = [
        pltpu.make_async_copy(src, dst, load.at[i])
        for i, (src, dst) in enumerate([
            (logits_hbm, logits_ref), (context_hbm, context_ref), (point_hbm, point_ref),
            (cell_hbm, cell_ref), (count_hbm, count_ref)])
    ]
    for copy in loads:
        copy.start()

    barrier = pltpu.get_barrier_semaphore()

    @pl.loop(1, strips)
    def _(step):
        pl.semaphore_signal(barrier, inc=1, device_id={"bev": lax.rem(me + step, strips)}, device_id_type=MESH)

    @pl.loop(1, scenes)
    def _(step):
        pl.semaphore_signal(barrier, inc=1, device_id={"scene": lax.rem(scene + step, scenes)}, device_id_type=MESH)

    loads[0].wait()
    logits = logits_ref[...]
    powers = jnp.exp(logits - jnp.max(logits, axis=0, keepdims=True))
    prob[...] = (powers / jnp.sum(powers, axis=0, keepdims=True)).astype(jnp.bfloat16)
    for copy in loads[1:]:
        copy.wait()
    pl.semaphore_wait(barrier, strips - 1 + scenes - 1)

    def context_copy(step):
        return pltpu.make_async_remote_copy(
            src_ref=context_ref, dst_ref=context_all.at[me],
            send_sem=ctx_send.at[step], recv_sem=ctx_recv.at[me],
            device_id={"bev": lax.rem(me + step, strips)}, device_id_type=MESH)

    def slot_copy(step):
        to = lax.rem(me + step, strips)
        return pltpu.make_async_remote_copy(
            src_ref=sent.at[to], dst_ref=got.at[me],
            send_sem=slot_send.at[step], recv_sem=slot_recv.at[me],
            device_id={"bev": to}, device_id_type=MESH)

    @pl.loop(1, strips)
    def _(step):
        context_copy(step).start()

    def hot_rows(count, ids):
        row = lax.broadcasted_iota(jnp.int32, (count, capacity), 0).astype(jnp.bfloat16)
        return jnp.where(row == ids.astype(jnp.bfloat16), jnp.bfloat16(1), jnp.bfloat16(0))

    depth_row = lax.broadcasted_iota(jnp.int32, (depth_bins, capacity), 0)
    slot_row = lax.broadcasted_iota(jnp.int32, (1, capacity), 1)

    def fill(to):
        points = point_ref[pl.ds(to, 1), :]
        live = slot_row < count_ref[0, to]
        pixel = points % pix_block
        depth = points // pix_block
        column = jnp.dot(prob[...], hot_rows(pix_block, pixel), preferred_element_type=jnp.float32)
        weight = jnp.sum(jnp.where(depth_row == depth, column, 0.0), axis=0, keepdims=True)
        weight = jnp.where(live, weight, 0.0)
        cell = jnp.where(live, cell_ref[pl.ds(to, 1), :], strip_cells)
        code = (cell * pix_block + pixel).astype(jnp.float32)
        for r in range(rows):
            sent[to, r:r + 1, :] = weight[:, r * LANES:(r + 1) * LANES]
            sent[to, rows + r:rows + r + 1, :] = code[:, r * LANES:(r + 1) * LANES]

    @pl.loop(1, strips)
    def _(step):
        fill(lax.rem(me + step, strips))
        slot_copy(step).start()

    fill(me)

    def line(block):
        return jnp.concatenate([block[r:r + 1, :] for r in range(rows)], axis=1)

    def scatter(half, cell, values):
        high = (cell // quarter) * sub + cell % sub - half * half_rows
        low = (cell // sub) % LOW
        spread = jnp.concatenate(
            [values * jnp.where(low == j, 1.0, 0.0).astype(jnp.bfloat16) for j in range(LOW)], axis=0)
        return lax.dot_general(
            spread, hot_rows(half_rows, high), (((1,), (1,)), ((), ())), preferred_element_type=jnp.float32)

    def form(features_map, slots, source, half):
        code = line(slots[rows:, :]).astype(jnp.int32)
        features = jnp.dot(features_map, hot_rows(pix_block, code % pix_block), preferred_element_type=jnp.float32)
        values = (features * line(slots[:rows, :])).astype(jnp.bfloat16)
        values_all[source] = values
        return scatter(half, code // pix_block, values)

    near = scene // group
    far = lax.rem(near + 1, HALVES)
    total[...] = form(context_ref[...], sent[me], me, far)

    @pl.loop(1, strips)
    def _(step):
        source = lax.rem(me + strips - step, strips)
        pltpu.make_async_remote_copy(
            src_ref=context_ref, dst_ref=context_all.at[source],
            send_sem=ctx_send.at[step], recv_sem=ctx_recv.at[source],
            device_id={"bev": source}, device_id_type=MESH).wait_recv()
        pltpu.make_async_remote_copy(
            src_ref=sent.at[source], dst_ref=got.at[source],
            send_sem=slot_send.at[step], recv_sem=slot_recv.at[source],
            device_id={"bev": source}, device_id_type=MESH).wait_recv()
        total[...] += form(context_all[source], got[source], source, far)

    def pack(half):
        for q in range(group):
            for j in range(LOW):
                parts[half * group + q, j] = total[
                    j * channels:(j + 1) * channels, q * sub:(q + 1) * sub].astype(jnp.bfloat16)

    def place(source):
        return out_ref.at[:, pl.ds(pl.multiple_of(source * channels, 16), channels), :]

    def part_copy(to):
        return pltpu.make_async_remote_copy(
            src_ref=parts.at[to], dst_ref=place(scene),
            send_sem=part_send.at[to], recv_sem=part_recv.at[scene],
            device_id={"scene": to}, device_id_type=MESH)

    pack(far)
    for q in range(group):
        part_copy(far * group + q).start()

    total[...] = scatter(near, line(sent[me][rows:, :]).astype(jnp.int32) // pix_block, values_all[me])

    @pl.loop(1, strips)
    def _(step):
        source = lax.rem(me + strips - step, strips)
        total[...] += scatter(near, line(got[source][rows:, :]).astype(jnp.int32) // pix_block, values_all[source])

    pack(near)
    others = [near * group + lax.rem(scene + o, group) for o in range(1, group)]
    for to in others:
        part_copy(to).start()
    out_ref[:, pl.ds(pl.multiple_of(scene * channels, 16), channels), :] = parts[scene]

    @pl.loop(1, strips)
    def _(step):
        context_copy(step).wait_send()
        slot_copy(step).wait_send()

    for to in [far * group + q for q in range(group)] + others:
        part_copy(to).wait_send()
        pltpu.make_async_remote_copy(
            src_ref=parts.at[to], dst_ref=place(to),
            send_sem=part_send.at[to], recv_sem=part_recv.at[to],
            device_id={"scene": to}, device_id_type=MESH).wait_recv()


def body(context, depth_logits, send_count, slot_point, slot_cell):
    strips = lax.axis_size("bev")
    scenes = lax.axis_size("scene")
    strip_cells = GRID * GRID // strips
    channels, pix_block = context.shape[1:]
    depth_bins = depth_logits.shape[1]
    capacity = slot_point.shape[3]
    quarter = strip_cells // scenes
    sub = quarter // LOW
    hbm = pl.BlockSpec(memory_space=pltpu.HBM)
    slots = (strips, 2 * capacity // LANES, LANES)
    pooled = pl.pallas_call(
        functools.partial(kernel, strips, scenes, strip_cells),
        out_shape=jax.ShapeDtypeStruct((LOW, scenes * channels, sub), jnp.bfloat16),
        in_specs=[hbm] * 5,
        out_specs=pl.BlockSpec(memory_space=pltpu.VMEM),
        scratch_shapes=[
            pltpu.VMEM((channels, pix_block), jnp.bfloat16),
            pltpu.VMEM((depth_bins, pix_block), jnp.float32),
            pltpu.SMEM((1, strips), jnp.int32),
            pltpu.VMEM((strips, capacity), jnp.int32),
            pltpu.VMEM((strips, capacity), jnp.int32),
            pltpu.VMEM((strips, channels, pix_block), jnp.bfloat16),
            pltpu.VMEM(slots, jnp.float32),
            pltpu.VMEM(slots, jnp.float32),
            pltpu.VMEM((depth_bins, pix_block), jnp.bfloat16),
            pltpu.VMEM((strips, channels, capacity), jnp.bfloat16),
            pltpu.VMEM((LOW * channels, scenes // HALVES * sub), jnp.float32),
            pltpu.VMEM((scenes, LOW, channels, sub), jnp.bfloat16),
            pltpu.SemaphoreType.DMA((5,)),
            pltpu.SemaphoreType.DMA((strips,)),
            pltpu.SemaphoreType.DMA((strips,)),
            pltpu.SemaphoreType.DMA((strips,)),
            pltpu.SemaphoreType.DMA((strips,)),
            pltpu.SemaphoreType.DMA((scenes,)),
            pltpu.SemaphoreType.DMA((scenes,)),
        ],
        compiler_params=pltpu.CompilerParams(
            collective_id=0, has_side_effects=True, vmem_limit_bytes=64 * 1024 * 1024),
    )(context[0], depth_logits[0], send_count[0], slot_point[0, 0], slot_cell[0, 0])
    return jnp.transpose(pooled, (0, 2, 1)).reshape(quarter, scenes * channels)


def solution(mesh):
    return jax.shard_map(
        body,
        mesh=mesh,
        in_specs=(
            P("scene", None, "bev"),
            P("scene", None, "bev"),
            P("scene", "bev", None),
            P("scene", "bev", None, None),
            P("scene", "bev", None, None),
        ),
        out_specs=P(("bev", "scene"), None),
        check_vma=False,
    )
```

```python
import functools

import jax
import jax.numpy as jnp
from jax import lax
from jax.experimental import pallas as pl
from jax.experimental.pallas import tpu as pltpu
from jax.sharding import PartitionSpec as P

GRID = 128
LANES = 128
LOW = 4
HALVES = 2
MESH = pl.DeviceIdType.MESH


def kernel(strips, scenes, strip_cells, context_hbm, logits_hbm, count_hbm, point_hbm, cell_hbm,
           out_ref, context_ref, logits_ref, count_ref, point_ref, cell_ref,
           context_all, sent, got, prob, row_ids, values_all, total, parts,
           load, ctx_send, ctx_recv, slot_send, slot_recv, part_send, part_recv):
    channels, pix_block = context_ref.shape
    depth_bins = logits_ref.shape[0]
    capacity = point_ref.shape[1]
    rows = capacity // LANES
    quarter = strip_cells // scenes
    sub = quarter // LOW
    group = scenes // HALVES
    half_rows = group * sub
    assert pix_block <= 256 and half_rows <= 256
    me = lax.axis_index("bev")
    scene = lax.axis_index("scene")

    loads = [
        pltpu.make_async_copy(src, dst, load.at[i])
        for i, (src, dst) in enumerate([
            (logits_hbm, logits_ref), (context_hbm, context_ref), (point_hbm, point_ref),
            (cell_hbm, cell_ref), (count_hbm, count_ref)])
    ]
    for copy in loads:
        copy.start()

    barrier = pltpu.get_barrier_semaphore()

    @pl.loop(1, strips)
    def _(step):
        pl.semaphore_signal(barrier, inc=1, device_id={"bev": lax.rem(me + step, strips)}, device_id_type=MESH)

    @pl.loop(1, scenes)
    def _(step):
        pl.semaphore_signal(barrier, inc=1, device_id={"scene": lax.rem(scene + step, scenes)}, device_id_type=MESH)

    loads[0].wait()
    logits = logits_ref[...]
    powers = jnp.exp(logits - jnp.max(logits, axis=0, keepdims=True))
    prob[...] = (powers / jnp.sum(powers, axis=0, keepdims=True)).astype(jnp.bfloat16)
    for copy in loads[1:]:
        copy.wait()
    pl.semaphore_wait(barrier, strips - 1 + scenes - 1)

    pair = me + 1 - 2 * lax.rem(me, 2)
    half_strips = strips // 2

    def target(item):
        start = jnp.where(item < half_strips, me, pair)
        return lax.rem(start + 2 * lax.rem(item, half_strips), strips)

    def origin(item):
        start = jnp.where(item < half_strips, me, pair)
        return lax.rem(start + strips - 2 * lax.rem(item, half_strips), strips)

    def own_context(item):
        return pltpu.make_async_remote_copy(
            src_ref=context_ref, dst_ref=context_all.at[me],
            send_sem=ctx_send.at[item], recv_sem=ctx_recv.at[me],
            device_id={"bev": target(item)}, device_id_type=MESH)

    def passed_context(item):
        source = origin(item)
        return pltpu.make_async_remote_copy(
            src_ref=context_all.at[source], dst_ref=context_all.at[source],
            send_sem=ctx_send.at[half_strips + item], recv_sem=ctx_recv.at[source],
            device_id={"bev": pair}, device_id_type=MESH)

    def context_arrived(item):
        source = origin(item)
        pltpu.make_async_remote_copy(
            src_ref=context_ref, dst_ref=context_all.at[source],
            send_sem=ctx_send.at[item], recv_sem=ctx_recv.at[source],
            device_id={"bev": source}, device_id_type=MESH).wait_recv()

    def slot_copy(item):
        to = target(item)
        return pltpu.make_async_remote_copy(
            src_ref=sent.at[to], dst_ref=got.at[me],
            send_sem=slot_send.at[item], recv_sem=slot_recv.at[me],
            device_id={"bev": to}, device_id_type=MESH)

    def slots_arrived(item):
        source = origin(item)
        pltpu.make_async_remote_copy(
            src_ref=sent.at[source], dst_ref=got.at[source],
            send_sem=slot_send.at[item], recv_sem=slot_recv.at[source],
            device_id={"bev": source}, device_id_type=MESH).wait_recv()

    @pl.loop(1, half_strips + 1)
    def _(item):
        own_context(item).start()

    context_all[me] = context_ref[...]
    row_ids[...] = lax.broadcasted_iota(jnp.int32, row_ids.shape, 0).astype(jnp.bfloat16)

    def hot_rows(count, ids):
        row = jnp.concatenate([row_ids[:count, :]] * (ids.shape[1] // LANES), axis=1)
        return jnp.where(row == ids.astype(jnp.bfloat16), jnp.bfloat16(1), jnp.bfloat16(0))

    depth_row = lax.broadcasted_iota(jnp.int32, (depth_bins, capacity), 0)
    slot_row = lax.broadcasted_iota(jnp.int32, (1, capacity), 1)

    def fill(to, slots, place):
        points = point_ref[pl.ds(to, 1), :]
        live = slot_row < count_ref[0, to]
        pixel = points % pix_block
        depth = points // pix_block
        column = jnp.dot(prob[...], hot_rows(pix_block, pixel), preferred_element_type=jnp.float32)
        weight = jnp.sum(jnp.where(depth_row == depth, column, 0.0), axis=0, keepdims=True)
        weight = jnp.where(live, weight, 0.0)
        cell = jnp.where(live, cell_ref[pl.ds(to, 1), :], strip_cells)
        code = (cell * pix_block + pixel).astype(jnp.float32)
        for r in range(rows):
            slots[place, r:r + 1, :] = weight[:, r * LANES:(r + 1) * LANES]
            slots[place, rows + r:rows + r + 1, :] = code[:, r * LANES:(r + 1) * LANES]

    def fill_two(group):
        for item in (2 * group + 1, 2 * group + 2):
            fill(target(item), sent, target(item))
        for item in (2 * group + 1, 2 * group + 2):
            slot_copy(item).start()

    def pass_on(item):
        context_arrived(item)
        passed_context(item).start()

    fill_two(0)
    fill_two(1)

    @pl.loop(1, half_strips - 2)
    def _(item):
        pass_on(item)
        fill_two(item + 1)

    pass_on(half_strips - 2)
    fill(target(strips - 1), sent, target(strips - 1))
    slot_copy(strips - 1).start()
    fill(me, got, me)
    pass_on(half_strips - 1)

    def line(block):
        return jnp.concatenate([block[r:r + 1, :] for r in range(rows)], axis=1)

    def scatter(half, cell, values):
        high = (cell // quarter) * sub + cell % sub - half * half_rows
        low = (cell // sub) % LOW
        spread = jnp.concatenate(
            [values * jnp.where(low == j, 1.0, 0.0).astype(jnp.bfloat16) for j in range(LOW)], axis=0)
        return lax.dot_general(
            spread, hot_rows(half_rows, high), (((1,), (1,)), ((), ())), preferred_element_type=jnp.float32)

    def codes(source):
        return line(got[source][rows:, :]).astype(jnp.int32)

    def form(source):
        code = codes(source)
        features = jnp.dot(
            context_all[source], hot_rows(pix_block, code % pix_block), preferred_element_type=jnp.float32)
        values = (features * line(got[source][:rows, :])).astype(jnp.bfloat16)
        values_all[source] = values
        return code // pix_block, values

    near = scene // group
    far = lax.rem(near + 1, HALVES)

    def form_two(first):
        made = [form(origin(item)) for item in (first, first + 1)]
        return scatter(far, jnp.concatenate([cell for cell, _ in made], axis=1),
                       jnp.concatenate([values for _, values in made], axis=1))

    slots_arrived(1)
    total[...] = form_two(0)

    @pl.loop(1, half_strips // 2)
    def _(step):
        slots_arrived(2 * step)
        slots_arrived(2 * step + 1)
        total[...] += form_two(2 * step)

    @pl.loop(half_strips // 2, half_strips)
    def _(step):
        for item in (2 * step, 2 * step + 1):
            slots_arrived(item)
            context_arrived(item)
        total[...] += form_two(2 * step)

    def pack(half):
        for q in range(group):
            for j in range(LOW):
                parts[half * group + q, :, j * sub:(j + 1) * sub] = total[
                    j * channels:(j + 1) * channels, q * sub:(q + 1) * sub].astype(jnp.bfloat16)

    def place(source):
        return out_ref.at[pl.ds(pl.multiple_of(source * channels, 16), channels), :]

    def part_copy(to):
        return pltpu.make_async_remote_copy(
            src_ref=parts.at[to], dst_ref=place(scene),
            send_sem=part_send.at[to], recv_sem=part_recv.at[scene],
            device_id={"scene": to}, device_id_type=MESH)

    pack(far)
    for q in range(group):
        part_copy(far * group + q).start()

    def again(first):
        sources = [2 * first, 2 * first + 1]
        return scatter(near, jnp.concatenate([codes(source) // pix_block for source in sources], axis=1),
                       jnp.concatenate([values_all[source] for source in sources], axis=1))

    total[...] = again(0)

    @pl.loop(1, half_strips)
    def _(step):
        total[...] += again(step)

    pack(near)
    others = [near * group + lax.rem(scene + o, group) for o in range(1, group)]
    for to in others:
        part_copy(to).start()
    out_ref[pl.ds(pl.multiple_of(scene * channels, 16), channels), :] = parts[scene]

    @pl.loop(1, strips)
    def _(step):
        slot_copy(step).wait_send()

    @pl.loop(1, half_strips + 1)
    def _(item):
        own_context(item).wait_send()

    @pl.loop(1, half_strips)
    def _(item):
        passed_context(item).wait_send()

    for to in [far * group + q for q in range(group)] + others:
        part_copy(to).wait_send()
        pltpu.make_async_remote_copy(
            src_ref=parts.at[to], dst_ref=place(to),
            send_sem=part_send.at[to], recv_sem=part_recv.at[to],
            device_id={"scene": to}, device_id_type=MESH).wait_recv()


def body(context, depth_logits, send_count, slot_point, slot_cell):
    strips = lax.axis_size("bev")
    scenes = lax.axis_size("scene")
    strip_cells = GRID * GRID // strips
    channels, pix_block = context.shape[1:]
    depth_bins = depth_logits.shape[1]
    capacity = slot_point.shape[3]
    quarter = strip_cells // scenes
    sub = quarter // LOW
    hbm = pl.BlockSpec(memory_space=pltpu.HBM)
    slots = (strips, 2 * capacity // LANES, LANES)
    pooled = pl.pallas_call(
        functools.partial(kernel, strips, scenes, strip_cells),
        out_shape=jax.ShapeDtypeStruct((scenes * channels, quarter), jnp.bfloat16),
        in_specs=[hbm] * 5,
        out_specs=pl.BlockSpec(memory_space=pltpu.VMEM),
        scratch_shapes=[
            pltpu.VMEM((channels, pix_block), jnp.bfloat16),
            pltpu.VMEM((depth_bins, pix_block), jnp.float32),
            pltpu.SMEM((1, strips), jnp.int32),
            pltpu.VMEM((strips, capacity), jnp.int32),
            pltpu.VMEM((strips, capacity), jnp.int32),
            pltpu.VMEM((strips, channels, pix_block), jnp.bfloat16),
            pltpu.VMEM(slots, jnp.float32),
            pltpu.VMEM(slots, jnp.float32),
            pltpu.VMEM((depth_bins, pix_block), jnp.bfloat16),
            pltpu.VMEM((256, LANES), jnp.bfloat16),
            pltpu.VMEM((strips, channels, capacity), jnp.bfloat16),
            pltpu.VMEM((LOW * channels, scenes // HALVES * sub), jnp.float32),
            pltpu.VMEM((scenes, channels, quarter), jnp.bfloat16),
            pltpu.SemaphoreType.DMA((5,)),
            pltpu.SemaphoreType.DMA((strips,)),
            pltpu.SemaphoreType.DMA((strips,)),
            pltpu.SemaphoreType.DMA((strips,)),
            pltpu.SemaphoreType.DMA((strips,)),
            pltpu.SemaphoreType.DMA((scenes,)),
            pltpu.SemaphoreType.DMA((scenes,)),
        ],
        compiler_params=pltpu.CompilerParams(
            collective_id=0, has_side_effects=True, vmem_limit_bytes=64 * 1024 * 1024),
    )(context[0], depth_logits[0], send_count[0], slot_point[0, 0], slot_cell[0, 0])
    return jnp.transpose(pooled)


def solution(mesh):
    return jax.shard_map(
        body,
        mesh=mesh,
        in_specs=(
            P("scene", None, "bev"),
            P("scene", None, "bev"),
            P("scene", "bev", None),
            P("scene", "bev", None, None),
            P("scene", "bev", None, None),
        ),
        out_specs=P(("bev", "scene"), None),
        check_vma=False,
    )
```

```python
import functools

import jax
import jax.numpy as jnp
from jax import lax
from jax.experimental import pallas as pl
from jax.experimental.pallas import tpu as pltpu
from jax.sharding import PartitionSpec as P

GRID = 128
LANES = 128
LOW = 4
HALVES = 2
MESH = pl.DeviceIdType.MESH


def kernel(strips, scenes, strip_cells, context_hbm, logits_hbm, count_hbm, point_hbm, cell_hbm,
           out_ref, context_ref, logits_ref, count_ref, point_ref, cell_ref,
           context_all, sent, got, prob, row_ids, values_all, total, parts,
           load, ctx_send, ctx_recv, slot_send, slot_recv, part_send, part_recv):
    channels, pix_block = context_ref.shape
    depth_bins = logits_ref.shape[0]
    capacity = point_ref.shape[1]
    rows = capacity // LANES
    quarter = strip_cells // scenes
    sub = quarter // LOW
    group = scenes // HALVES
    half_rows = group * sub
    assert pix_block <= 256 and half_rows <= 256
    me = lax.axis_index("bev")
    scene = lax.axis_index("scene")

    loads = [
        pltpu.make_async_copy(src, dst, load.at[i])
        for i, (src, dst) in enumerate([
            (logits_hbm, logits_ref), (context_hbm, context_ref), (point_hbm, point_ref),
            (cell_hbm, cell_ref), (count_hbm, count_ref)])
    ]
    for copy in loads:
        copy.start()

    barrier = pltpu.get_barrier_semaphore()

    @pl.loop(1, strips)
    def _(step):
        pl.semaphore_signal(barrier, inc=1, device_id={"bev": lax.rem(me + step, strips)}, device_id_type=MESH)

    @pl.loop(1, scenes)
    def _(step):
        pl.semaphore_signal(barrier, inc=1, device_id={"scene": lax.rem(scene + step, scenes)}, device_id_type=MESH)

    pl.semaphore_wait(barrier, strips - 1 + scenes - 1)

    pair = me + 1 - 2 * lax.rem(me, 2)
    half_strips = strips // 2

    def target(item):
        start = jnp.where(item < half_strips, me, pair)
        return lax.rem(start + 2 * lax.rem(item, half_strips), strips)

    def origin(item):
        start = jnp.where(item < half_strips, me, pair)
        return lax.rem(start + strips - 2 * lax.rem(item, half_strips), strips)

    def own_context(item):
        return pltpu.make_async_remote_copy(
            src_ref=context_hbm, dst_ref=context_all.at[me],
            send_sem=ctx_send.at[item], recv_sem=ctx_recv.at[me],
            device_id={"bev": target(item)}, device_id_type=MESH)

    def passed_context(item):
        source = origin(item)
        return pltpu.make_async_remote_copy(
            src_ref=context_all.at[source], dst_ref=context_all.at[source],
            send_sem=ctx_send.at[half_strips + item], recv_sem=ctx_recv.at[source],
            device_id={"bev": pair}, device_id_type=MESH)

    def context_arrived(item):
        source = origin(item)
        pltpu.make_async_remote_copy(
            src_ref=context_ref, dst_ref=context_all.at[source],
            send_sem=ctx_send.at[item], recv_sem=ctx_recv.at[source],
            device_id={"bev": source}, device_id_type=MESH).wait_recv()

    def slot_copy(item):
        to = target(item)
        return pltpu.make_async_remote_copy(
            src_ref=sent.at[to], dst_ref=got.at[me],
            send_sem=slot_send.at[item], recv_sem=slot_recv.at[me],
            device_id={"bev": to}, device_id_type=MESH)

    def slots_arrived(item):
        source = origin(item)
        pltpu.make_async_remote_copy(
            src_ref=sent.at[source], dst_ref=got.at[source],
            send_sem=slot_send.at[item], recv_sem=slot_recv.at[source],
            device_id={"bev": source}, device_id_type=MESH).wait_recv()

    @pl.loop(1, half_strips + 1)
    def _(item):
        own_context(item).start()

    loads[0].wait()
    logits = logits_ref[...]
    powers = jnp.exp(logits - jnp.max(logits, axis=0, keepdims=True))
    prob[...] = (powers / jnp.sum(powers, axis=0, keepdims=True)).astype(jnp.bfloat16)
    for copy in loads[1:]:
        copy.wait()
    context_all[me] = context_ref[...]
    row_ids[...] = lax.broadcasted_iota(jnp.int32, row_ids.shape, 0).astype(jnp.bfloat16)

    def hot_rows(count, ids):
        row = jnp.concatenate([row_ids[:count, :]] * (ids.shape[1] // LANES), axis=1)
        return jnp.where(row == ids.astype(jnp.bfloat16), jnp.bfloat16(1), jnp.bfloat16(0))

    depth_row = lax.broadcasted_iota(jnp.int32, (depth_bins, capacity), 0)
    slot_row = lax.broadcasted_iota(jnp.int32, (1, capacity), 1)

    def fill(to, slots, place):
        points = point_ref[pl.ds(to, 1), :]
        live = slot_row < count_ref[0, to]
        pixel = points % pix_block
        depth = points // pix_block
        column = jnp.dot(prob[...], hot_rows(pix_block, pixel), preferred_element_type=jnp.float32)
        weight = jnp.sum(jnp.where(depth_row == depth, column, 0.0), axis=0, keepdims=True)
        weight = jnp.where(live, weight, 0.0)
        cell = jnp.where(live, cell_ref[pl.ds(to, 1), :], strip_cells)
        code = (cell * pix_block + pixel).astype(jnp.float32)
        for r in range(rows):
            slots[place, r:r + 1, :] = weight[:, r * LANES:(r + 1) * LANES]
            slots[place, rows + r:rows + r + 1, :] = code[:, r * LANES:(r + 1) * LANES]

    def fill_two(group):
        for item in (2 * group + 1, 2 * group + 2):
            fill(target(item), sent, target(item))
        for item in (2 * group + 1, 2 * group + 2):
            slot_copy(item).start()

    def pass_on(item):
        context_arrived(item)
        passed_context(item).start()

    fill_two(0)
    fill_two(1)

    @pl.loop(1, half_strips - 2)
    def _(item):
        pass_on(item)
        fill_two(item + 1)

    pass_on(half_strips - 2)
    fill(target(strips - 1), sent, target(strips - 1))
    slot_copy(strips - 1).start()
    fill(me, got, me)
    pass_on(half_strips - 1)

    def line(block):
        return jnp.concatenate([block[r:r + 1, :] for r in range(rows)], axis=1)

    def scatter(half, cell, values):
        high = (cell // quarter) * sub + cell % sub - half * half_rows
        low = (cell // sub) % LOW
        spread = jnp.concatenate(
            [values * jnp.where(low == j, 1.0, 0.0).astype(jnp.bfloat16) for j in range(LOW)], axis=0)
        return lax.dot_general(
            spread, hot_rows(half_rows, high), (((1,), (1,)), ((), ())), preferred_element_type=jnp.float32)

    def codes(source):
        return line(got[source][rows:, :]).astype(jnp.int32)

    def form(source):
        code = codes(source)
        features = jnp.dot(
            context_all[source], hot_rows(pix_block, code % pix_block), preferred_element_type=jnp.float32)
        values = (features * line(got[source][:rows, :])).astype(jnp.bfloat16)
        values_all[source] = values
        return code // pix_block, values

    near = scene // group
    far = lax.rem(near + 1, HALVES)

    def form_two(first):
        made = [form(origin(item)) for item in (first, first + 1)]
        return scatter(far, jnp.concatenate([cell for cell, _ in made], axis=1),
                       jnp.concatenate([values for _, values in made], axis=1))

    slots_arrived(1)
    total[...] = form_two(0)

    @pl.loop(1, half_strips // 2)
    def _(step):
        slots_arrived(2 * step)
        slots_arrived(2 * step + 1)
        total[...] += form_two(2 * step)

    @pl.loop(half_strips // 2, half_strips)
    def _(step):
        for item in (2 * step, 2 * step + 1):
            slots_arrived(item)
            context_arrived(item)
        total[...] += form_two(2 * step)

    def pack(half):
        for q in range(group):
            for j in range(LOW):
                parts[half * group + q, :, j * sub:(j + 1) * sub] = total[
                    j * channels:(j + 1) * channels, q * sub:(q + 1) * sub].astype(jnp.bfloat16)

    def place(source):
        return out_ref.at[pl.ds(pl.multiple_of(source * channels, 16), channels), :]

    def part_copy(to):
        return pltpu.make_async_remote_copy(
            src_ref=parts.at[to], dst_ref=place(scene),
            send_sem=part_send.at[to], recv_sem=part_recv.at[scene],
            device_id={"scene": to}, device_id_type=MESH)

    pack(far)
    for q in range(group):
        part_copy(far * group + q).start()

    def again(first):
        sources = [2 * first, 2 * first + 1]
        return scatter(near, jnp.concatenate([codes(source) // pix_block for source in sources], axis=1),
                       jnp.concatenate([values_all[source] for source in sources], axis=1))

    total[...] = again(0)

    @pl.loop(1, half_strips)
    def _(step):
        total[...] += again(step)

    pack(near)
    others = [near * group + lax.rem(scene + o, group) for o in range(1, group)]
    for to in others:
        part_copy(to).start()
    out_ref[pl.ds(pl.multiple_of(scene * channels, 16), channels), :] = parts[scene]

    @pl.loop(1, strips)
    def _(step):
        slot_copy(step).wait_send()

    @pl.loop(1, half_strips + 1)
    def _(item):
        own_context(item).wait_send()

    @pl.loop(1, half_strips)
    def _(item):
        passed_context(item).wait_send()

    for to in [far * group + q for q in range(group)] + others:
        part_copy(to).wait_send()
        pltpu.make_async_remote_copy(
            src_ref=parts.at[to], dst_ref=place(to),
            send_sem=part_send.at[to], recv_sem=part_recv.at[to],
            device_id={"scene": to}, device_id_type=MESH).wait_recv()


def body(context, depth_logits, send_count, slot_point, slot_cell):
    strips = lax.axis_size("bev")
    scenes = lax.axis_size("scene")
    strip_cells = GRID * GRID // strips
    channels, pix_block = context.shape[1:]
    depth_bins = depth_logits.shape[1]
    capacity = slot_point.shape[3]
    quarter = strip_cells // scenes
    sub = quarter // LOW
    hbm = pl.BlockSpec(memory_space=pltpu.HBM)
    slots = (strips, 2 * capacity // LANES, LANES)
    pooled = pl.pallas_call(
        functools.partial(kernel, strips, scenes, strip_cells),
        out_shape=pltpu.VMEM((scenes * channels, quarter), jnp.bfloat16),
        in_specs=[hbm] * 5,
        out_specs=pl.BlockSpec(memory_space=pltpu.VMEM),
        scratch_shapes=[
            pltpu.VMEM((channels, pix_block), jnp.bfloat16),
            pltpu.VMEM((depth_bins, pix_block), jnp.float32),
            pltpu.SMEM((1, strips), jnp.int32),
            pltpu.VMEM((strips, capacity), jnp.int32),
            pltpu.VMEM((strips, capacity), jnp.int32),
            pltpu.VMEM((strips, channels, pix_block), jnp.bfloat16),
            pltpu.VMEM(slots, jnp.float32),
            pltpu.VMEM(slots, jnp.float32),
            pltpu.VMEM((depth_bins, pix_block), jnp.bfloat16),
            pltpu.VMEM((256, LANES), jnp.bfloat16),
            pltpu.VMEM((strips, channels, capacity), jnp.bfloat16),
            pltpu.VMEM((LOW * channels, scenes // HALVES * sub), jnp.float32),
            pltpu.VMEM((scenes, channels, quarter), jnp.bfloat16),
            pltpu.SemaphoreType.DMA((5,)),
            pltpu.SemaphoreType.DMA((strips,)),
            pltpu.SemaphoreType.DMA((strips,)),
            pltpu.SemaphoreType.DMA((strips,)),
            pltpu.SemaphoreType.DMA((strips,)),
            pltpu.SemaphoreType.DMA((scenes,)),
            pltpu.SemaphoreType.DMA((scenes,)),
        ],
        compiler_params=pltpu.CompilerParams(
            collective_id=0, has_side_effects=True, vmem_limit_bytes=63 * 1024 * 1024),
    )(context[0], depth_logits[0], send_count[0], slot_point[0, 0], slot_cell[0, 0])
    return jnp.transpose(pooled)


def solution(mesh):
    return jax.shard_map(
        body,
        mesh=mesh,
        in_specs=(
            P("scene", None, "bev"),
            P("scene", None, "bev"),
            P("scene", "bev", None),
            P("scene", "bev", None, None),
            P("scene", "bev", None, None),
        ),
        out_specs=P(("bev", "scene"), None),
        check_vma=False,
    )
```

```python
import functools

import jax
import jax.numpy as jnp
from jax import lax
from jax.experimental import pallas as pl
from jax.experimental.pallas import tpu as pltpu
from jax.sharding import PartitionSpec as P

GRID = 128
LANES = 128
LOW = 4
HALVES = 2
MESH = pl.DeviceIdType.MESH


def log2(size):
    assert size & (size - 1) == 0
    return size.bit_length() - 1


def kernel(strips, scenes, strip_cells, context_hbm, logits_hbm, count_hbm, point_hbm, cell_hbm,
           out_ref, context_ref, logits_ref, count_ref, point_ref, cell_ref, depth_table, code_table,
           context_all, sent, got, prob, row_ids, values_all, total, parts,
           load, ctx_send, ctx_recv, slot_send, slot_recv, part_send, part_recv):
    channels, pix_block = context_ref.shape
    depth_bins = logits_ref.shape[0]
    capacity = point_ref.shape[1]
    rows = capacity // LANES
    quarter = strip_cells // scenes
    sub = quarter // LOW
    group = scenes // HALVES
    half_rows = group * sub
    assert pix_block <= 256 and half_rows <= 256
    me = lax.axis_index("bev")
    scene = lax.axis_index("scene")

    loads = [
        pltpu.make_async_copy(src, dst, load.at[i])
        for i, (src, dst) in enumerate([
            (logits_hbm, logits_ref), (context_hbm, context_ref), (point_hbm, point_ref),
            (cell_hbm, cell_ref), (count_hbm, count_ref)])
    ]
    for copy in loads:
        copy.start()

    barrier = pltpu.get_barrier_semaphore()

    @pl.loop(1, strips)
    def _(step):
        pl.semaphore_signal(barrier, inc=1, device_id={"bev": lax.rem(me + step, strips)}, device_id_type=MESH)

    @pl.loop(1, scenes)
    def _(step):
        pl.semaphore_signal(barrier, inc=1, device_id={"scene": lax.rem(scene + step, scenes)}, device_id_type=MESH)

    pl.semaphore_wait(barrier, strips - 1 + scenes - 1)

    pair = me + 1 - 2 * lax.rem(me, 2)
    half_strips = strips // 2

    def target(item):
        start = jnp.where(item < half_strips, me, pair)
        return lax.rem(start + 2 * lax.rem(item, half_strips), strips)

    def origin(item):
        start = jnp.where(item < half_strips, me, pair)
        return lax.rem(start + strips - 2 * lax.rem(item, half_strips), strips)

    def own_context(item):
        return pltpu.make_async_remote_copy(
            src_ref=context_hbm, dst_ref=context_all.at[me],
            send_sem=ctx_send.at[item], recv_sem=ctx_recv.at[me],
            device_id={"bev": target(item)}, device_id_type=MESH)

    def passed_context(item):
        source = origin(item)
        return pltpu.make_async_remote_copy(
            src_ref=context_all.at[source], dst_ref=context_all.at[source],
            send_sem=ctx_send.at[half_strips + item], recv_sem=ctx_recv.at[source],
            device_id={"bev": pair}, device_id_type=MESH)

    def context_arrived(item):
        source = origin(item)
        pltpu.make_async_remote_copy(
            src_ref=context_ref, dst_ref=context_all.at[source],
            send_sem=ctx_send.at[item], recv_sem=ctx_recv.at[source],
            device_id={"bev": source}, device_id_type=MESH).wait_recv()

    def slot_copy(item):
        to = target(item)
        return pltpu.make_async_remote_copy(
            src_ref=sent.at[to], dst_ref=got.at[me],
            send_sem=slot_send.at[item], recv_sem=slot_recv.at[me],
            device_id={"bev": to}, device_id_type=MESH)

    def slots_arrived(item):
        source = origin(item)
        pltpu.make_async_remote_copy(
            src_ref=sent.at[source], dst_ref=got.at[source],
            send_sem=slot_send.at[item], recv_sem=slot_recv.at[source],
            device_id={"bev": source}, device_id_type=MESH).wait_recv()

    @pl.loop(1, half_strips + 1)
    def _(item):
        own_context(item).start()

    loads[0].wait()
    logits = logits_ref[...]
    powers = jnp.exp(logits - jnp.max(logits, axis=0, keepdims=True))
    prob[...] = (powers / jnp.sum(powers, axis=0, keepdims=True)).astype(jnp.bfloat16)
    for copy in loads[1:]:
        copy.wait()
    context_all[me] = context_ref[...]
    row_ids[...] = lax.broadcasted_iota(jnp.int32, row_ids.shape, 0).astype(jnp.bfloat16)

    def hot_rows(count, ids):
        row = jnp.concatenate([row_ids[:count, :]] * (ids.shape[1] // LANES), axis=1)
        return jnp.where(row == ids.astype(jnp.bfloat16), jnp.bfloat16(1), jnp.bfloat16(0))

    points = point_ref[...]
    target_row = lax.broadcasted_iota(jnp.int32, points.shape, 0)
    counts = jnp.zeros_like(points)
    for d in range(strips):
        counts = jnp.where(target_row == d, count_ref[0, d], counts)
    live = lax.broadcasted_iota(jnp.int32, points.shape, 1) < counts
    pixels = points & (pix_block - 1)
    cells = jnp.where(live, cell_ref[...], strip_cells)
    point_ref[...] = pixels
    depth_table[...] = jnp.where(live, points >> log2(pix_block), depth_bins)
    code_table[...] = ((cells << log2(pix_block)) + pixels).astype(jnp.float32)
    depth_row = lax.broadcasted_iota(jnp.int32, (depth_bins, capacity), 0)

    def fill(to, slots, place):
        column = jnp.dot(prob[...], hot_rows(pix_block, point_ref[pl.ds(to, 1), :]),
                         preferred_element_type=jnp.float32)
        depth = depth_table[pl.ds(to, 1), :]
        weight = jnp.sum(jnp.where(depth_row == depth, column, 0.0), axis=0, keepdims=True)
        code = code_table[pl.ds(to, 1), :]
        for r in range(rows):
            slots[place, r:r + 1, :] = weight[:, r * LANES:(r + 1) * LANES]
            slots[place, rows + r:rows + r + 1, :] = code[:, r * LANES:(r + 1) * LANES]

    def fill_two(group):
        for item in (2 * group + 1, 2 * group + 2):
            fill(target(item), sent, target(item))
        for item in (2 * group + 1, 2 * group + 2):
            slot_copy(item).start()

    def pass_on(item):
        context_arrived(item)
        passed_context(item).start()

    fill_two(0)
    fill_two(1)

    @pl.loop(1, half_strips - 2)
    def _(item):
        pass_on(item)
        fill_two(item + 1)

    pass_on(half_strips - 2)
    fill(target(strips - 1), sent, target(strips - 1))
    slot_copy(strips - 1).start()
    fill(me, got, me)
    pass_on(half_strips - 1)

    def line(block):
        return jnp.concatenate([block[r:r + 1, :] for r in range(rows)], axis=1)

    def decode(source):
        code = got[source][rows:, :].astype(jnp.int32)
        return code & (pix_block - 1), code >> log2(pix_block)

    def scatter(half, cells, values):
        high = [((cell >> log2(quarter)) << log2(sub)) + (cell & (sub - 1)) - half * half_rows for cell in cells]
        low = [(cell >> log2(sub)) & (LOW - 1) for cell in cells]
        high = jnp.concatenate([line(block) for block in high], axis=1)
        low = jnp.concatenate([line(block) for block in low], axis=1).astype(jnp.bfloat16)
        values = jnp.concatenate(values, axis=1)
        low = jnp.broadcast_to(low, values.shape)
        spread = jnp.concatenate(
            [jnp.where(low == jnp.bfloat16(j), values, jnp.bfloat16(0)) for j in range(LOW)], axis=0)
        return lax.dot_general(
            spread, hot_rows(half_rows, high), (((1,), (1,)), ((), ())), preferred_element_type=jnp.float32)

    def form(source):
        pixel, cell = decode(source)
        features = jnp.dot(
            context_all[source], hot_rows(pix_block, line(pixel)), preferred_element_type=jnp.float32)
        values = (features * line(got[source][:rows, :])).astype(jnp.bfloat16)
        values_all[source] = values
        return cell, values

    near = scene // group
    far = lax.rem(near + 1, HALVES)

    def form_two(first):
        made = [form(origin(item)) for item in (first, first + 1)]
        return scatter(far, [cell for cell, _ in made], [values for _, values in made])

    slots_arrived(1)
    total[...] = form_two(0)

    @pl.loop(1, half_strips // 2)
    def _(step):
        slots_arrived(2 * step)
        slots_arrived(2 * step + 1)
        total[...] += form_two(2 * step)

    @pl.loop(half_strips // 2, half_strips)
    def _(step):
        for item in (2 * step, 2 * step + 1):
            slots_arrived(item)
            context_arrived(item)
        total[...] += form_two(2 * step)

    def pack(half):
        for q in range(group):
            for j in range(LOW):
                parts[half * group + q, :, j * sub:(j + 1) * sub] = total[
                    j * channels:(j + 1) * channels, q * sub:(q + 1) * sub].astype(jnp.bfloat16)

    def place(source):
        return out_ref.at[pl.ds(pl.multiple_of(source * channels, 16), channels), :]

    def part_copy(to):
        return pltpu.make_async_remote_copy(
            src_ref=parts.at[to], dst_ref=place(scene),
            send_sem=part_send.at[to], recv_sem=part_recv.at[scene],
            device_id={"scene": to}, device_id_type=MESH)

    pack(far)
    for q in range(group):
        part_copy(far * group + q).start()

    def again(first):
        sources = [2 * first, 2 * first + 1]
        return scatter(near, [decode(source)[1] for source in sources], [values_all[source] for source in sources])

    total[...] = again(0)

    @pl.loop(1, half_strips)
    def _(step):
        total[...] += again(step)

    pack(near)
    others = [near * group + lax.rem(scene + o, group) for o in range(1, group)]
    for to in others:
        part_copy(to).start()
    out_ref[pl.ds(pl.multiple_of(scene * channels, 16), channels), :] = parts[scene]

    @pl.loop(1, strips)
    def _(step):
        slot_copy(step).wait_send()

    @pl.loop(1, half_strips + 1)
    def _(item):
        own_context(item).wait_send()

    @pl.loop(1, half_strips)
    def _(item):
        passed_context(item).wait_send()

    for to in [far * group + q for q in range(group)] + others:
        part_copy(to).wait_send()
        pltpu.make_async_remote_copy(
            src_ref=parts.at[to], dst_ref=place(to),
            send_sem=part_send.at[to], recv_sem=part_recv.at[to],
            device_id={"scene": to}, device_id_type=MESH).wait_recv()


def body(context, depth_logits, send_count, slot_point, slot_cell):
    strips = lax.axis_size("bev")
    scenes = lax.axis_size("scene")
    strip_cells = GRID * GRID // strips
    channels, pix_block = context.shape[1:]
    depth_bins = depth_logits.shape[1]
    capacity = slot_point.shape[3]
    quarter = strip_cells // scenes
    sub = quarter // LOW
    hbm = pl.BlockSpec(memory_space=pltpu.HBM)
    slots = (strips, 2 * capacity // LANES, LANES)
    pooled = pl.pallas_call(
        functools.partial(kernel, strips, scenes, strip_cells),
        out_shape=pltpu.VMEM((scenes * channels, quarter), jnp.bfloat16),
        in_specs=[hbm] * 5,
        out_specs=pl.BlockSpec(memory_space=pltpu.VMEM),
        scratch_shapes=[
            pltpu.VMEM((channels, pix_block), jnp.bfloat16),
            pltpu.VMEM((depth_bins, pix_block), jnp.float32),
            pltpu.SMEM((1, strips), jnp.int32),
            pltpu.VMEM((strips, capacity), jnp.int32),
            pltpu.VMEM((strips, capacity), jnp.int32),
            pltpu.VMEM((strips, capacity), jnp.int32),
            pltpu.VMEM((strips, capacity), jnp.float32),
            pltpu.VMEM((strips, channels, pix_block), jnp.bfloat16),
            pltpu.VMEM(slots, jnp.float32),
            pltpu.VMEM(slots, jnp.float32),
            pltpu.VMEM((depth_bins, pix_block), jnp.bfloat16),
            pltpu.VMEM((256, LANES), jnp.bfloat16),
            pltpu.VMEM((strips, channels, capacity), jnp.bfloat16),
            pltpu.VMEM((LOW * channels, scenes // HALVES * sub), jnp.float32),
            pltpu.VMEM((scenes, channels, quarter), jnp.bfloat16),
            pltpu.SemaphoreType.DMA((5,)),
            pltpu.SemaphoreType.DMA((strips,)),
            pltpu.SemaphoreType.DMA((strips,)),
            pltpu.SemaphoreType.DMA((strips,)),
            pltpu.SemaphoreType.DMA((strips,)),
            pltpu.SemaphoreType.DMA((scenes,)),
            pltpu.SemaphoreType.DMA((scenes,)),
        ],
        compiler_params=pltpu.CompilerParams(
            collective_id=0, has_side_effects=True, vmem_limit_bytes=63 * 1024 * 1024),
    )(context[0], depth_logits[0], send_count[0], slot_point[0, 0], slot_cell[0, 0])
    return jnp.transpose(pooled)


def solution(mesh):
    return jax.shard_map(
        body,
        mesh=mesh,
        in_specs=(
            P("scene", None, "bev"),
            P("scene", None, "bev"),
            P("scene", "bev", None),
            P("scene", "bev", None, None),
            P("scene", "bev", None, None),
        ),
        out_specs=P(("bev", "scene"), None),
        check_vma=False,
    )
```

```python
import functools

import jax
import jax.numpy as jnp
from jax import lax
from jax.experimental import pallas as pl
from jax.experimental.pallas import tpu as pltpu
from jax.sharding import PartitionSpec as P

GRID = 128
LANES = 128
LOW = 4
HALVES = 2
MESH = pl.DeviceIdType.MESH


def log2(size):
    assert size & (size - 1) == 0
    return size.bit_length() - 1


def kernel(strips, scenes, strip_cells, context_hbm, logits_hbm, count_hbm, point_hbm, cell_hbm,
           out_ref, context_ref, logits_ref, count_ref, point_ref, cell_ref, depth_table, code_table,
           context_all, sent, got, prob, row_ids, values_all, total, parts,
           load, ctx_send, ctx_recv, slot_send, slot_recv, part_send, part_recv):
    channels, pix_block = context_ref.shape
    depth_bins = logits_ref.shape[0]
    capacity = point_ref.shape[1]
    rows = capacity // LANES
    quarter = strip_cells // scenes
    sub = quarter // LOW
    group = scenes // HALVES
    half_rows = group * sub
    assert pix_block <= 256 and half_rows <= 256
    me = lax.axis_index("bev")
    scene = lax.axis_index("scene")

    barrier = pltpu.get_barrier_semaphore()

    @pl.loop(1, strips)
    def _(step):
        pl.semaphore_signal(barrier, inc=1, device_id={"bev": lax.rem(me + step, strips)}, device_id_type=MESH)

    @pl.loop(1, scenes)
    def _(step):
        pl.semaphore_signal(barrier, inc=1, device_id={"scene": lax.rem(scene + step, scenes)}, device_id_type=MESH)

    loads = [
        pltpu.make_async_copy(src, dst, load.at[i])
        for i, (src, dst) in enumerate([
            (logits_hbm, logits_ref), (context_hbm, context_ref), (point_hbm, point_ref),
            (cell_hbm, cell_ref), (count_hbm, count_ref)])
    ]
    for copy in loads:
        copy.start()

    pl.semaphore_wait(barrier, strips - 1 + scenes - 1)

    pair = me + 1 - 2 * lax.rem(me, 2)
    half_strips = strips // 2

    def target(item):
        start = jnp.where(item < half_strips, me, pair)
        return lax.rem(start + 2 * lax.rem(item, half_strips), strips)

    def origin(item):
        start = jnp.where(item < half_strips, me, pair)
        return lax.rem(start + strips - 2 * lax.rem(item, half_strips), strips)

    def own_context(item):
        return pltpu.make_async_remote_copy(
            src_ref=context_hbm, dst_ref=context_all.at[me],
            send_sem=ctx_send.at[item], recv_sem=ctx_recv.at[me],
            device_id={"bev": target(item)}, device_id_type=MESH)

    def passed_context(item):
        source = origin(item)
        return pltpu.make_async_remote_copy(
            src_ref=context_all.at[source], dst_ref=context_all.at[source],
            send_sem=ctx_send.at[half_strips + item], recv_sem=ctx_recv.at[source],
            device_id={"bev": pair}, device_id_type=MESH)

    def context_arrived(item):
        source = origin(item)
        pltpu.make_async_remote_copy(
            src_ref=context_ref, dst_ref=context_all.at[source],
            send_sem=ctx_send.at[item], recv_sem=ctx_recv.at[source],
            device_id={"bev": source}, device_id_type=MESH).wait_recv()

    def slot_copy(item):
        to = target(item)
        return pltpu.make_async_remote_copy(
            src_ref=sent.at[to], dst_ref=got.at[me],
            send_sem=slot_send.at[item], recv_sem=slot_recv.at[me],
            device_id={"bev": to}, device_id_type=MESH)

    def slots_arrived(item):
        source = origin(item)
        pltpu.make_async_remote_copy(
            src_ref=sent.at[source], dst_ref=got.at[source],
            send_sem=slot_send.at[item], recv_sem=slot_recv.at[source],
            device_id={"bev": source}, device_id_type=MESH).wait_recv()

    own_context(half_strips).start()

    @pl.loop(1, half_strips)
    def _(item):
        own_context(item).start()

    loads[0].wait()
    logits = logits_ref[...]
    powers = jnp.exp(logits - jnp.max(logits, axis=0, keepdims=True))
    prob[...] = (powers / jnp.sum(powers, axis=0, keepdims=True)).astype(jnp.bfloat16)
    for copy in loads[1:]:
        copy.wait()
    context_all[me] = context_ref[...]
    row_ids[...] = lax.broadcasted_iota(jnp.int32, row_ids.shape, 0).astype(jnp.bfloat16)

    def hot_rows(count, ids):
        row = jnp.concatenate([row_ids[:count, :]] * (ids.shape[1] // LANES), axis=1)
        return jnp.where(row == ids.astype(jnp.bfloat16), jnp.bfloat16(1), jnp.bfloat16(0))

    points = point_ref[...]
    target_row = lax.broadcasted_iota(jnp.int32, points.shape, 0)
    counts = jnp.zeros_like(points)
    for d in range(strips):
        counts = jnp.where(target_row == d, count_ref[0, d], counts)
    live = lax.broadcasted_iota(jnp.int32, points.shape, 1) < counts
    pixels = points & (pix_block - 1)
    cells = jnp.where(live, cell_ref[...], strip_cells)
    point_ref[...] = pixels
    depth_table[...] = jnp.where(live, points >> log2(pix_block), depth_bins)
    code_table[...] = ((cells << log2(pix_block)) + pixels).astype(jnp.float32)
    depth_row = lax.broadcasted_iota(jnp.int32, (depth_bins, capacity), 0)

    def fill(to, slots, place):
        column = jnp.dot(prob[...], hot_rows(pix_block, point_ref[pl.ds(to, 1), :]),
                         preferred_element_type=jnp.float32)
        depth = depth_table[pl.ds(to, 1), :]
        weight = jnp.sum(jnp.where(depth_row == depth, column, 0.0), axis=0, keepdims=True)
        code = code_table[pl.ds(to, 1), :]
        for r in range(rows):
            slots[place, r:r + 1, :] = weight[:, r * LANES:(r + 1) * LANES]
            slots[place, rows + r:rows + r + 1, :] = code[:, r * LANES:(r + 1) * LANES]

    def fill_two(group):
        for item in (2 * group + 1, 2 * group + 2):
            fill(target(item), sent, target(item))
        for item in (2 * group + 1, 2 * group + 2):
            slot_copy(item).start()

    def pass_on(item):
        context_arrived(item)
        passed_context(item).start()

    @pl.loop(0, half_strips - 1)
    def _(step):
        fill_two(step)

    fill(target(strips - 1), sent, target(strips - 1))
    slot_copy(strips - 1).start()
    fill(me, got, me)

    def line(block):
        return jnp.concatenate([block[r:r + 1, :] for r in range(rows)], axis=1)

    def decode(source):
        code = got[source][rows:, :].astype(jnp.int32)
        return code & (pix_block - 1), code >> log2(pix_block)

    def scatter(half, cells, values):
        high = [((cell >> log2(quarter)) << log2(sub)) + (cell & (sub - 1)) - half * half_rows for cell in cells]
        low = [(cell >> log2(sub)) & (LOW - 1) for cell in cells]
        high = jnp.concatenate([line(block) for block in high], axis=1)
        low = jnp.concatenate([line(block) for block in low], axis=1).astype(jnp.bfloat16)
        values = jnp.concatenate(values, axis=1)
        low = jnp.broadcast_to(low, values.shape)
        spread = jnp.concatenate(
            [jnp.where(low == jnp.bfloat16(j), values, jnp.bfloat16(0)) for j in range(LOW)], axis=0)
        return lax.dot_general(
            spread, hot_rows(half_rows, high), (((1,), (1,)), ((), ())), preferred_element_type=jnp.float32)

    def form(source):
        pixel, cell = decode(source)
        features = jnp.dot(
            context_all[source], hot_rows(pix_block, line(pixel)), preferred_element_type=jnp.float32)
        values = (features * line(got[source][:rows, :])).astype(jnp.bfloat16)
        values_all[source] = values
        return cell, values

    near = scene // group
    far = lax.rem(near + 1, HALVES)

    def pool(*items):
        made = [form(origin(item)) for item in items]
        return scatter(far, [cell for cell, _ in made], [values for _, values in made])

    def arrived(item):
        slots_arrived(item)

        @pl.when(item >= half_strips)
        def _():
            context_arrived(item)

    total[...] = pool(0)

    @pl.loop(1, half_strips)
    def _(item):
        pass_on(item)

    @pl.loop(0, half_strips - 1)
    def _(step):
        arrived(2 * step + 1)
        arrived(2 * step + 2)
        total[...] += pool(2 * step + 1, 2 * step + 2)

    arrived(strips - 1)
    total[...] += pool(strips - 1)

    def pack(half):
        for q in range(group):
            for j in range(LOW):
                parts[half * group + q, :, j * sub:(j + 1) * sub] = total[
                    j * channels:(j + 1) * channels, q * sub:(q + 1) * sub].astype(jnp.bfloat16)

    def place(source):
        return out_ref.at[pl.ds(pl.multiple_of(source * channels, 16), channels), :]

    def part_copy(to):
        return pltpu.make_async_remote_copy(
            src_ref=parts.at[to], dst_ref=place(scene),
            send_sem=part_send.at[to], recv_sem=part_recv.at[scene],
            device_id={"scene": to}, device_id_type=MESH)

    pack(far)
    for q in range(group):
        part_copy(far * group + q).start()

    def again(first):
        sources = [2 * first, 2 * first + 1]
        return scatter(near, [decode(source)[1] for source in sources], [values_all[source] for source in sources])

    total[...] = again(0)

    @pl.loop(1, half_strips)
    def _(step):
        total[...] += again(step)

    pack(near)
    others = [near * group + lax.rem(scene + o, group) for o in range(1, group)]
    for to in others:
        part_copy(to).start()
    out_ref[pl.ds(pl.multiple_of(scene * channels, 16), channels), :] = parts[scene]

    @pl.loop(1, strips)
    def _(step):
        slot_copy(step).wait_send()

    @pl.loop(1, half_strips + 1)
    def _(item):
        own_context(item).wait_send()

    @pl.loop(1, half_strips)
    def _(item):
        passed_context(item).wait_send()

    for to in [far * group + q for q in range(group)] + others:
        part_copy(to).wait_send()
        pltpu.make_async_remote_copy(
            src_ref=parts.at[to], dst_ref=place(to),
            send_sem=part_send.at[to], recv_sem=part_recv.at[to],
            device_id={"scene": to}, device_id_type=MESH).wait_recv()


def body(context, depth_logits, send_count, slot_point, slot_cell):
    strips = lax.axis_size("bev")
    scenes = lax.axis_size("scene")
    strip_cells = GRID * GRID // strips
    channels, pix_block = context.shape[1:]
    depth_bins = depth_logits.shape[1]
    capacity = slot_point.shape[3]
    quarter = strip_cells // scenes
    sub = quarter // LOW
    hbm = pl.BlockSpec(memory_space=pltpu.HBM)
    slots = (strips, 2 * capacity // LANES, LANES)
    pooled = pl.pallas_call(
        functools.partial(kernel, strips, scenes, strip_cells),
        out_shape=pltpu.VMEM((scenes * channels, quarter), jnp.bfloat16),
        in_specs=[hbm] * 5,
        out_specs=pl.BlockSpec(memory_space=pltpu.VMEM),
        scratch_shapes=[
            pltpu.VMEM((channels, pix_block), jnp.bfloat16),
            pltpu.VMEM((depth_bins, pix_block), jnp.float32),
            pltpu.SMEM((1, strips), jnp.int32),
            pltpu.VMEM((strips, capacity), jnp.int32),
            pltpu.VMEM((strips, capacity), jnp.int32),
            pltpu.VMEM((strips, capacity), jnp.int32),
            pltpu.VMEM((strips, capacity), jnp.float32),
            pltpu.VMEM((strips, channels, pix_block), jnp.bfloat16),
            pltpu.VMEM(slots, jnp.float32),
            pltpu.VMEM(slots, jnp.float32),
            pltpu.VMEM((depth_bins, pix_block), jnp.bfloat16),
            pltpu.VMEM((256, LANES), jnp.bfloat16),
            pltpu.VMEM((strips, channels, capacity), jnp.bfloat16),
            pltpu.VMEM((LOW * channels, scenes // HALVES * sub), jnp.float32),
            pltpu.VMEM((scenes, channels, quarter), jnp.bfloat16),
            pltpu.SemaphoreType.DMA((5,)),
            pltpu.SemaphoreType.DMA((strips,)),
            pltpu.SemaphoreType.DMA((strips,)),
            pltpu.SemaphoreType.DMA((strips,)),
            pltpu.SemaphoreType.DMA((strips,)),
            pltpu.SemaphoreType.DMA((scenes,)),
            pltpu.SemaphoreType.DMA((scenes,)),
        ],
        compiler_params=pltpu.CompilerParams(
            collective_id=0, has_side_effects=True, vmem_limit_bytes=63 * 1024 * 1024),
    )(context[0], depth_logits[0], send_count[0], slot_point[0, 0], slot_cell[0, 0])
    return jnp.transpose(pooled)


def solution(mesh):
    return jax.shard_map(
        body,
        mesh=mesh,
        in_specs=(
            P("scene", None, "bev"),
            P("scene", None, "bev"),
            P("scene", "bev", None),
            P("scene", "bev", None, None),
            P("scene", "bev", None, None),
        ),
        out_specs=P(("bev", "scene"), None),
        check_vma=False,
    )
```

```python
import functools

import jax
import jax.numpy as jnp
from jax import lax
from jax.experimental import pallas as pl
from jax.experimental.pallas import tpu as pltpu
from jax.sharding import PartitionSpec as P

GRID = 128
LANES = 128
LOW = 4
HALVES = 2
MESH = pl.DeviceIdType.MESH


def log2(size):
    assert size & (size - 1) == 0
    return size.bit_length() - 1


def kernel(strips, scenes, strip_cells, context_hbm, logits_hbm, count_hbm, point_hbm, cell_hbm,
           out_ref, context_ref, logits_ref, count_ref, point_ref, cell_ref, depth_table, code_table,
           context_all, sent, got, prob, row_ids, values_all, total, parts,
           load, ctx_send, ctx_recv, slot_send, slot_recv, part_send, part_recv):
    channels, pix_block = context_ref.shape
    depth_bins = logits_ref.shape[0]
    capacity = point_ref.shape[1]
    rows = capacity // LANES
    quarter = strip_cells // scenes
    sub = quarter // LOW
    group = scenes // HALVES
    half_rows = group * sub
    assert pix_block <= 256 and half_rows <= 256
    me = lax.axis_index("bev")
    scene = lax.axis_index("scene")

    barrier = pltpu.get_barrier_semaphore()

    @pl.loop(1, strips)
    def _(step):
        pl.semaphore_signal(barrier, inc=1, device_id={"bev": lax.rem(me + step, strips)}, device_id_type=MESH)

    @pl.loop(1, scenes)
    def _(step):
        pl.semaphore_signal(barrier, inc=1, device_id={"scene": lax.rem(scene + step, scenes)}, device_id_type=MESH)

    loads = [
        pltpu.make_async_copy(src, dst, load.at[i])
        for i, (src, dst) in enumerate([
            (logits_hbm, logits_ref), (context_hbm, context_ref), (point_hbm, point_ref),
            (cell_hbm, cell_ref), (count_hbm, count_ref)])
    ]
    for copy in loads:
        copy.start()

    pl.semaphore_wait(barrier, strips - 1 + scenes - 1)

    pair = me + 1 - 2 * lax.rem(me, 2)
    half_strips = strips // 2

    def target(item):
        item = jnp.int32(item)
        key = 2 * lax.rem(item, half_strips) + lax.div(item, half_strips)
        place = jnp.int32(0)
        for bit in range(log2(strips)):
            mine = lax.rem(lax.div(me, 2 ** bit), 2)
            other = lax.rem(lax.div(key, 2 ** bit), 2)
            place = place + (mine + other - 2 * mine * other) * 2 ** bit
        return place

    origin = target

    def own_context(item):
        return pltpu.make_async_remote_copy(
            src_ref=context_hbm, dst_ref=context_all.at[me],
            send_sem=ctx_send.at[item], recv_sem=ctx_recv.at[me],
            device_id={"bev": target(item)}, device_id_type=MESH)

    def passed_context(item):
        source = origin(item)
        return pltpu.make_async_remote_copy(
            src_ref=context_all.at[source], dst_ref=context_all.at[source],
            send_sem=ctx_send.at[half_strips + item], recv_sem=ctx_recv.at[source],
            device_id={"bev": pair}, device_id_type=MESH)

    def context_arrived(item):
        source = origin(item)
        pltpu.make_async_remote_copy(
            src_ref=context_ref, dst_ref=context_all.at[source],
            send_sem=ctx_send.at[item], recv_sem=ctx_recv.at[source],
            device_id={"bev": source}, device_id_type=MESH).wait_recv()

    def slot_copy(item):
        to = target(item)
        return pltpu.make_async_remote_copy(
            src_ref=sent.at[to], dst_ref=got.at[me],
            send_sem=slot_send.at[item], recv_sem=slot_recv.at[me],
            device_id={"bev": to}, device_id_type=MESH)

    def slots_arrived(item):
        source = origin(item)
        pltpu.make_async_remote_copy(
            src_ref=sent.at[source], dst_ref=got.at[source],
            send_sem=slot_send.at[item], recv_sem=slot_recv.at[source],
            device_id={"bev": source}, device_id_type=MESH).wait_recv()

    own_context(half_strips).start()

    @pl.loop(1, half_strips)
    def _(item):
        own_context(item).start()

    loads[0].wait()
    logits = logits_ref[...]
    powers = jnp.exp(logits - jnp.max(logits, axis=0, keepdims=True))
    prob[...] = (powers / jnp.sum(powers, axis=0, keepdims=True)).astype(jnp.bfloat16)
    for copy in loads[1:]:
        copy.wait()
    context_all[me] = context_ref[...]
    row_ids[...] = lax.broadcasted_iota(jnp.int32, row_ids.shape, 0).astype(jnp.bfloat16)

    def hot_rows(count, ids):
        row = jnp.concatenate([row_ids[:count, :]] * (ids.shape[1] // LANES), axis=1)
        return jnp.where(row == ids.astype(jnp.bfloat16), jnp.bfloat16(1), jnp.bfloat16(0))

    points = point_ref[...]
    target_row = lax.broadcasted_iota(jnp.int32, points.shape, 0)
    counts = jnp.zeros_like(points)
    for d in range(strips):
        counts = jnp.where(target_row == d, count_ref[0, d], counts)
    live = lax.broadcasted_iota(jnp.int32, points.shape, 1) < counts
    pixels = points & (pix_block - 1)
    cells = jnp.where(live, cell_ref[...], strip_cells)
    point_ref[...] = pixels
    depth_table[...] = jnp.where(live, points >> log2(pix_block), depth_bins)
    code_table[...] = ((cells << log2(pix_block)) + pixels).astype(jnp.float32)
    depth_row = lax.broadcasted_iota(jnp.int32, (depth_bins, capacity), 0)

    def fill(to, slots, place):
        column = jnp.dot(prob[...], hot_rows(pix_block, point_ref[pl.ds(to, 1), :]),
                         preferred_element_type=jnp.float32)
        depth = depth_table[pl.ds(to, 1), :]
        weight = jnp.sum(jnp.where(depth_row == depth, column, 0.0), axis=0, keepdims=True)
        code = code_table[pl.ds(to, 1), :]
        for r in range(rows):
            slots[place, r:r + 1, :] = weight[:, r * LANES:(r + 1) * LANES]
            slots[place, rows + r:rows + r + 1, :] = code[:, r * LANES:(r + 1) * LANES]

    def fill_two(group):
        for item in (2 * group + 1, 2 * group + 2):
            fill(target(item), sent, target(item))
        for item in (2 * group + 1, 2 * group + 2):
            slot_copy(item).start()

    def pass_on(item):
        context_arrived(item)
        passed_context(item).start()

    @pl.loop(1, half_strips)
    def _(item):
        fill_two(item - 1)
        pass_on(item)

    fill(target(strips - 1), sent, target(strips - 1))
    slot_copy(strips - 1).start()
    fill(me, got, me)

    def line(block):
        return jnp.concatenate([block[r:r + 1, :] for r in range(rows)], axis=1)

    def decode(source):
        code = got[source][rows:, :].astype(jnp.int32)
        return code & (pix_block - 1), code >> log2(pix_block)

    def scatter(half, cells, values):
        high = [((cell >> log2(quarter)) << log2(sub)) + (cell & (sub - 1)) - half * half_rows for cell in cells]
        low = [(cell >> log2(sub)) & (LOW - 1) for cell in cells]
        high = jnp.concatenate([line(block) for block in high], axis=1)
        low = jnp.concatenate([line(block) for block in low], axis=1).astype(jnp.bfloat16)
        values = jnp.concatenate(values, axis=1)
        low = jnp.broadcast_to(low, values.shape)
        spread = jnp.concatenate(
            [jnp.where(low == jnp.bfloat16(j), values, jnp.bfloat16(0)) for j in range(LOW)], axis=0)
        return lax.dot_general(
            spread, hot_rows(half_rows, high), (((1,), (1,)), ((), ())), preferred_element_type=jnp.float32)

    def form(source):
        pixel, cell = decode(source)
        features = jnp.dot(
            context_all[source], hot_rows(pix_block, line(pixel)), preferred_element_type=jnp.float32)
        values = (features * line(got[source][:rows, :])).astype(jnp.bfloat16)
        values_all[source] = values
        return cell, values

    near = scene // group
    far = lax.rem(near + 1, HALVES)

    def pool(*items):
        made = [form(origin(item)) for item in items]
        return scatter(far, [cell for cell, _ in made], [values for _, values in made])

    def arrived(item):
        slots_arrived(item)

        @pl.when(item >= half_strips)
        def _():
            context_arrived(item)

    total[...] = pool(0)

    @pl.loop(0, half_strips - 1)
    def _(step):
        arrived(2 * step + 1)
        arrived(2 * step + 2)
        total[...] += pool(2 * step + 1, 2 * step + 2)

    arrived(strips - 1)
    total[...] += pool(strips - 1)

    def pack(half):
        for q in range(group):
            for j in range(LOW):
                parts[half * group + q, :, j * sub:(j + 1) * sub] = total[
                    j * channels:(j + 1) * channels, q * sub:(q + 1) * sub].astype(jnp.bfloat16)

    def place(source):
        return out_ref.at[pl.ds(pl.multiple_of(source * channels, 16), channels), :]

    def part_copy(to):
        return pltpu.make_async_remote_copy(
            src_ref=parts.at[to], dst_ref=place(scene),
            send_sem=part_send.at[to], recv_sem=part_recv.at[scene],
            device_id={"scene": to}, device_id_type=MESH)

    pack(far)
    for q in range(group):
        part_copy(far * group + q).start()

    def again(first):
        sources = [2 * first, 2 * first + 1]
        return scatter(near, [decode(source)[1] for source in sources], [values_all[source] for source in sources])

    total[...] = again(0)

    @pl.loop(1, half_strips)
    def _(step):
        total[...] += again(step)

    pack(near)
    others = [near * group + lax.rem(scene + o, group) for o in range(1, group)]
    for to in others:
        part_copy(to).start()
    out_ref[pl.ds(pl.multiple_of(scene * channels, 16), channels), :] = parts[scene]

    @pl.loop(1, strips)
    def _(step):
        slot_copy(step).wait_send()

    @pl.loop(1, half_strips + 1)
    def _(item):
        own_context(item).wait_send()

    @pl.loop(1, half_strips)
    def _(item):
        passed_context(item).wait_send()

    for to in [far * group + q for q in range(group)] + others:
        part_copy(to).wait_send()
        pltpu.make_async_remote_copy(
            src_ref=parts.at[to], dst_ref=place(to),
            send_sem=part_send.at[to], recv_sem=part_recv.at[to],
            device_id={"scene": to}, device_id_type=MESH).wait_recv()


def body(context, depth_logits, send_count, slot_point, slot_cell):
    strips = lax.axis_size("bev")
    scenes = lax.axis_size("scene")
    strip_cells = GRID * GRID // strips
    channels, pix_block = context.shape[1:]
    depth_bins = depth_logits.shape[1]
    capacity = slot_point.shape[3]
    quarter = strip_cells // scenes
    sub = quarter // LOW
    hbm = pl.BlockSpec(memory_space=pltpu.HBM)
    slots = (strips, 2 * capacity // LANES, LANES)
    pooled = pl.pallas_call(
        functools.partial(kernel, strips, scenes, strip_cells),
        out_shape=pltpu.VMEM((scenes * channels, quarter), jnp.bfloat16),
        in_specs=[hbm] * 5,
        out_specs=pl.BlockSpec(memory_space=pltpu.VMEM),
        scratch_shapes=[
            pltpu.VMEM((channels, pix_block), jnp.bfloat16),
            pltpu.VMEM((depth_bins, pix_block), jnp.float32),
            pltpu.SMEM((1, strips), jnp.int32),
            pltpu.VMEM((strips, capacity), jnp.int32),
            pltpu.VMEM((strips, capacity), jnp.int32),
            pltpu.VMEM((strips, capacity), jnp.int32),
            pltpu.VMEM((strips, capacity), jnp.float32),
            pltpu.VMEM((strips, channels, pix_block), jnp.bfloat16),
            pltpu.VMEM(slots, jnp.float32),
            pltpu.VMEM(slots, jnp.float32),
            pltpu.VMEM((depth_bins, pix_block), jnp.bfloat16),
            pltpu.VMEM((256, LANES), jnp.bfloat16),
            pltpu.VMEM((strips, channels, capacity), jnp.bfloat16),
            pltpu.VMEM((LOW * channels, scenes // HALVES * sub), jnp.float32),
            pltpu.VMEM((scenes, channels, quarter), jnp.bfloat16),
            pltpu.SemaphoreType.DMA((5,)),
            pltpu.SemaphoreType.DMA((strips,)),
            pltpu.SemaphoreType.DMA((strips,)),
            pltpu.SemaphoreType.DMA((strips,)),
            pltpu.SemaphoreType.DMA((strips,)),
            pltpu.SemaphoreType.DMA((scenes,)),
            pltpu.SemaphoreType.DMA((scenes,)),
        ],
        compiler_params=pltpu.CompilerParams(
            collective_id=0, has_side_effects=True, vmem_limit_bytes=63 * 1024 * 1024),
    )(context[0], depth_logits[0], send_count[0], slot_point[0, 0], slot_cell[0, 0])
    return jnp.transpose(pooled)


def solution(mesh):
    return jax.shard_map(
        body,
        mesh=mesh,
        in_specs=(
            P("scene", None, "bev"),
            P("scene", None, "bev"),
            P("scene", "bev", None),
            P("scene", "bev", None, None),
            P("scene", "bev", None, None),
        ),
        out_specs=P(("bev", "scene"), None),
        check_vma=False,
    )
```

```python
import functools

import jax
import jax.numpy as jnp
from jax import lax
from jax.experimental import pallas as pl
from jax.experimental.pallas import tpu as pltpu
from jax.sharding import PartitionSpec as P

GRID = 128
LANES = 128
LOW = 4
HALVES = 2
BLOCK = 4
MESH = pl.DeviceIdType.MESH


def log2(size):
    assert size & (size - 1) == 0
    return size.bit_length() - 1


def kernel(strips, scenes, strip_cells, context_hbm, logits_hbm, count_hbm, point_hbm, cell_hbm,
           out_ref, context_ref, logits_ref, count_ref, point_ref, cell_ref, depth_table, code_table,
           context_all, sent, got, prob, row_ids, values_all, total, parts,
           load, ctx_send, ctx_recv, slot_send, slot_recv, part_send, part_recv):
    channels, pix_block = context_ref.shape
    depth_bins = logits_ref.shape[0]
    capacity = point_ref.shape[1]
    rows = capacity // LANES
    quarter = strip_cells // scenes
    sub = quarter // LOW
    group = scenes // HALVES
    half_rows = group * sub
    assert pix_block <= 256 and half_rows <= 256
    me = lax.axis_index("bev")
    scene = lax.axis_index("scene")

    loads = [
        pltpu.make_async_copy(src, dst, load.at[i])
        for i, (src, dst) in enumerate([
            (logits_hbm, logits_ref), (context_hbm, context_ref), (point_hbm, point_ref),
            (cell_hbm, cell_ref), (count_hbm, count_ref)])
    ]
    for copy in loads:
        copy.start()

    barrier = pltpu.get_barrier_semaphore()

    @pl.loop(1, strips)
    def _(step):
        pl.semaphore_signal(barrier, inc=1, device_id={"bev": lax.rem(me + step, strips)}, device_id_type=MESH)

    @pl.loop(1, scenes)
    def _(step):
        pl.semaphore_signal(barrier, inc=1, device_id={"scene": lax.rem(scene + step, scenes)}, device_id_type=MESH)

    pl.semaphore_wait(barrier, strips - 1 + scenes - 1)

    pair = me + 1 - 2 * lax.rem(me, 2)
    half_strips = strips // 2

    def target(item):
        start = jnp.where(item < half_strips, me, pair)
        return lax.rem(start + 2 * lax.rem(item, half_strips), strips)

    def origin(item):
        start = jnp.where(item < half_strips, me, pair)
        return lax.rem(start + strips - 2 * lax.rem(item, half_strips), strips)

    def own_context(item):
        return pltpu.make_async_remote_copy(
            src_ref=context_hbm, dst_ref=context_all.at[me],
            send_sem=ctx_send.at[item], recv_sem=ctx_recv.at[me],
            device_id={"bev": target(item)}, device_id_type=MESH)

    def passed_context(item):
        source = origin(item)
        return pltpu.make_async_remote_copy(
            src_ref=context_all.at[source], dst_ref=context_all.at[source],
            send_sem=ctx_send.at[half_strips + item], recv_sem=ctx_recv.at[source],
            device_id={"bev": pair}, device_id_type=MESH)

    def context_arrived(item):
        source = origin(item)
        pltpu.make_async_remote_copy(
            src_ref=context_ref, dst_ref=context_all.at[source],
            send_sem=ctx_send.at[item], recv_sem=ctx_recv.at[source],
            device_id={"bev": source}, device_id_type=MESH).wait_recv()

    def slot_copy(item):
        to = target(item)
        return pltpu.make_async_remote_copy(
            src_ref=sent.at[to], dst_ref=got.at[me],
            send_sem=slot_send.at[item], recv_sem=slot_recv.at[me],
            device_id={"bev": to}, device_id_type=MESH)

    def slots_arrived(item):
        source = origin(item)
        pltpu.make_async_remote_copy(
            src_ref=sent.at[source], dst_ref=got.at[source],
            send_sem=slot_send.at[item], recv_sem=slot_recv.at[source],
            device_id={"bev": source}, device_id_type=MESH).wait_recv()

    @pl.loop(1, half_strips + 1)
    def _(item):
        own_context(item).start()

    loads[0].wait()
    logits = logits_ref[...]
    powers = jnp.exp(logits - jnp.max(logits, axis=0, keepdims=True))
    prob[...] = (powers / jnp.sum(powers, axis=0, keepdims=True)).astype(jnp.bfloat16)
    for copy in loads[1:]:
        copy.wait()
    context_all[me] = context_ref[...]
    row_ids[...] = lax.broadcasted_iota(jnp.int32, row_ids.shape, 0).astype(jnp.bfloat16)

    def hot_rows(count, ids):
        row = jnp.concatenate([row_ids[:count, :]] * (ids.shape[1] // LANES), axis=1)
        return jnp.where(row == ids.astype(jnp.bfloat16), jnp.bfloat16(1), jnp.bfloat16(0))

    points = point_ref[...]
    target_row = lax.broadcasted_iota(jnp.int32, points.shape, 0)
    counts = jnp.zeros_like(points)
    for d in range(strips):
        counts = jnp.where(target_row == d, count_ref[0, d], counts)
    live = lax.broadcasted_iota(jnp.int32, points.shape, 1) < counts
    pixels = points & (pix_block - 1)
    cells = jnp.where(live, cell_ref[...], strip_cells)
    point_ref[...] = pixels
    depth_table[...] = jnp.where(live, points >> log2(pix_block), depth_bins)
    code_table[...] = ((cells << log2(pix_block)) + pixels).astype(jnp.float32)
    depth_row = lax.broadcasted_iota(jnp.int32, (depth_bins, capacity), 0)

    def fill(to, slots, place):
        column = jnp.dot(prob[...], hot_rows(pix_block, point_ref[pl.ds(to, 1), :]),
                         preferred_element_type=jnp.float32)
        depth = depth_table[pl.ds(to, 1), :]
        weight = jnp.sum(jnp.where(depth_row == depth, column, 0.0), axis=0, keepdims=True)
        code = code_table[pl.ds(to, 1), :]
        for r in range(rows):
            slots[place, r:r + 1, :] = weight[:, r * LANES:(r + 1) * LANES]
            slots[place, rows + r:rows + r + 1, :] = code[:, r * LANES:(r + 1) * LANES]

    blocks = strips // BLOCK
    assert strips % (2 * BLOCK) == 0

    def fill_block(block, last):
        items = [block * BLOCK + i + 1 for i in range(BLOCK - last)]
        for item in items:
            fill(target(item), sent, target(item))
        if last:
            fill(me, got, me)
        for item in items:
            slot_copy(item).start()

    def pass_on(item):
        context_arrived(item)
        passed_context(item).start()

    @pl.loop(0, blocks - 1)
    def _(block):
        fill_block(block, 0)
        pass_on(block + 1)

    fill_block(blocks - 1, 1)

    @pl.loop(blocks, half_strips)
    def _(item):
        pass_on(item)

    def line(block):
        return jnp.concatenate([block[r:r + 1, :] for r in range(rows)], axis=1)

    def decode(source):
        code = got[source][rows:, :].astype(jnp.int32)
        return code & (pix_block - 1), code >> log2(pix_block)

    def scatter(half, cells, values):
        high = [((cell >> log2(quarter)) << log2(sub)) + (cell & (sub - 1)) - half * half_rows for cell in cells]
        low = [(cell >> log2(sub)) & (LOW - 1) for cell in cells]
        high = jnp.concatenate([line(block) for block in high], axis=1)
        low = jnp.concatenate([line(block) for block in low], axis=1).astype(jnp.bfloat16)
        values = jnp.concatenate(values, axis=1)
        low = jnp.broadcast_to(low, values.shape)
        spread = jnp.concatenate(
            [jnp.where(low == jnp.bfloat16(j), values, jnp.bfloat16(0)) for j in range(LOW)], axis=0)
        return lax.dot_general(
            spread, hot_rows(half_rows, high), (((1,), (1,)), ((), ())), preferred_element_type=jnp.float32)

    def form(source):
        pixel, cell = decode(source)
        features = jnp.dot(
            context_all[source], hot_rows(pix_block, line(pixel)), preferred_element_type=jnp.float32)
        values = (features * line(got[source][:rows, :])).astype(jnp.bfloat16)
        values_all[source] = values
        return cell, values

    near = scene // group
    far = lax.rem(near + 1, HALVES)

    def pool(block):
        made = [form(origin(block * BLOCK + i)) for i in range(BLOCK)]
        return scatter(far, [cell for cell, _ in made], [values for _, values in made])

    for item in range(1, BLOCK):
        slots_arrived(item)
    total[...] = pool(0)

    @pl.loop(1, blocks // 2)
    def _(block):
        for i in range(BLOCK):
            slots_arrived(block * BLOCK + i)
        total[...] += pool(block)

    @pl.loop(blocks // 2, blocks)
    def _(block):
        for i in range(BLOCK):
            slots_arrived(block * BLOCK + i)
            context_arrived(block * BLOCK + i)
        total[...] += pool(block)

    def pack(half):
        for q in range(group):
            for j in range(LOW):
                parts[half * group + q, :, j * sub:(j + 1) * sub] = total[
                    j * channels:(j + 1) * channels, q * sub:(q + 1) * sub].astype(jnp.bfloat16)

    def place(source):
        return out_ref.at[pl.ds(pl.multiple_of(source * channels, 16), channels), :]

    def part_copy(to):
        return pltpu.make_async_remote_copy(
            src_ref=parts.at[to], dst_ref=place(scene),
            send_sem=part_send.at[to], recv_sem=part_recv.at[scene],
            device_id={"scene": to}, device_id_type=MESH)

    pack(far)
    for q in range(group):
        part_copy(far * group + q).start()

    def again(block):
        sources = [2 * BLOCK * block + i for i in range(2 * BLOCK)]
        return scatter(near, [decode(source)[1] for source in sources], [values_all[source] for source in sources])

    total[...] = again(0)

    @pl.loop(1, blocks // 2)
    def _(block):
        total[...] += again(block)

    pack(near)
    others = [near * group + lax.rem(scene + o, group) for o in range(1, group)]
    for to in others:
        part_copy(to).start()
    out_ref[pl.ds(pl.multiple_of(scene * channels, 16), channels), :] = parts[scene]

    @pl.loop(1, strips)
    def _(step):
        slot_copy(step).wait_send()

    @pl.loop(1, half_strips + 1)
    def _(item):
        own_context(item).wait_send()

    @pl.loop(1, half_strips)
    def _(item):
        passed_context(item).wait_send()

    for to in [far * group + q for q in range(group)] + others:
        part_copy(to).wait_send()
        pltpu.make_async_remote_copy(
            src_ref=parts.at[to], dst_ref=place(to),
            send_sem=part_send.at[to], recv_sem=part_recv.at[to],
            device_id={"scene": to}, device_id_type=MESH).wait_recv()


def body(context, depth_logits, send_count, slot_point, slot_cell):
    strips = lax.axis_size("bev")
    scenes = lax.axis_size("scene")
    strip_cells = GRID * GRID // strips
    channels, pix_block = context.shape[1:]
    depth_bins = depth_logits.shape[1]
    capacity = slot_point.shape[3]
    quarter = strip_cells // scenes
    sub = quarter // LOW
    hbm = pl.BlockSpec(memory_space=pltpu.HBM)
    slots = (strips, 2 * capacity // LANES, LANES)
    pooled = pl.pallas_call(
        functools.partial(kernel, strips, scenes, strip_cells),
        out_shape=pltpu.VMEM((scenes * channels, quarter), jnp.bfloat16),
        in_specs=[hbm] * 5,
        out_specs=pl.BlockSpec(memory_space=pltpu.VMEM),
        scratch_shapes=[
            pltpu.VMEM((channels, pix_block), jnp.bfloat16),
            pltpu.VMEM((depth_bins, pix_block), jnp.float32),
            pltpu.SMEM((1, strips), jnp.int32),
            pltpu.VMEM((strips, capacity), jnp.int32),
            pltpu.VMEM((strips, capacity), jnp.int32),
            pltpu.VMEM((strips, capacity), jnp.int32),
            pltpu.VMEM((strips, capacity), jnp.float32),
            pltpu.VMEM((strips, channels, pix_block), jnp.bfloat16),
            pltpu.VMEM(slots, jnp.float32),
            pltpu.VMEM(slots, jnp.float32),
            pltpu.VMEM((depth_bins, pix_block), jnp.bfloat16),
            pltpu.VMEM((256, LANES), jnp.bfloat16),
            pltpu.VMEM((strips, channels, capacity), jnp.bfloat16),
            pltpu.VMEM((LOW * channels, scenes // HALVES * sub), jnp.float32),
            pltpu.VMEM((scenes, channels, quarter), jnp.bfloat16),
            pltpu.SemaphoreType.DMA((5,)),
            pltpu.SemaphoreType.DMA((strips,)),
            pltpu.SemaphoreType.DMA((strips,)),
            pltpu.SemaphoreType.DMA((strips,)),
            pltpu.SemaphoreType.DMA((strips,)),
            pltpu.SemaphoreType.DMA((scenes,)),
            pltpu.SemaphoreType.DMA((scenes,)),
        ],
        compiler_params=pltpu.CompilerParams(
            collective_id=0, has_side_effects=True, vmem_limit_bytes=63 * 1024 * 1024),
    )(context[0], depth_logits[0], send_count[0], slot_point[0, 0], slot_cell[0, 0])
    return jnp.transpose(pooled)


def solution(mesh):
    return jax.shard_map(
        body,
        mesh=mesh,
        in_specs=(
            P("scene", None, "bev"),
            P("scene", None, "bev"),
            P("scene", "bev", None),
            P("scene", "bev", None, None),
            P("scene", "bev", None, None),
        ),
        out_specs=P(("bev", "scene"), None),
        check_vma=False,
    )
```

```python
import functools

import jax
import jax.numpy as jnp
from jax import lax
from jax.experimental import pallas as pl
from jax.experimental.pallas import tpu as pltpu
from jax.sharding import PartitionSpec as P

GRID = 128
LANES = 128
LOW = 4
HALVES = 2
MESH = pl.DeviceIdType.MESH


def log2(size):
    assert size & (size - 1) == 0
    return size.bit_length() - 1


def kernel(strips, scenes, strip_cells, context_hbm, logits_hbm, count_hbm, point_hbm, cell_hbm,
           out_ref, context_ref, logits_ref, count_ref, point_ref, cell_ref, depth_table, code_table,
           context_all, sent, got, prob, row_ids, values_all, total, parts,
           load, ctx_send, ctx_recv, slot_send, slot_recv, part_send, part_recv):
    channels, pix_block = context_ref.shape
    depth_bins = logits_ref.shape[0]
    capacity = point_ref.shape[1]
    rows = capacity // LANES
    quarter = strip_cells // scenes
    sub = quarter // LOW
    group = scenes // HALVES
    half_rows = group * sub
    assert pix_block <= 256 and half_rows <= 256
    me = lax.axis_index("bev")
    scene = lax.axis_index("scene")

    barrier = pltpu.get_barrier_semaphore()

    @pl.loop(1, strips)
    def _(step):
        pl.semaphore_signal(barrier, inc=1, device_id={"bev": lax.rem(me + step, strips)}, device_id_type=MESH)

    @pl.loop(1, scenes)
    def _(step):
        pl.semaphore_signal(barrier, inc=1, device_id={"scene": lax.rem(scene + step, scenes)}, device_id_type=MESH)

    loads = [
        pltpu.make_async_copy(src, dst, load.at[i])
        for i, (src, dst) in enumerate([
            (logits_hbm, logits_ref), (context_hbm, context_ref), (point_hbm, point_ref),
            (cell_hbm, cell_ref), (count_hbm, count_ref)])
    ]
    for copy in loads:
        copy.start()

    pl.semaphore_wait(barrier, strips - 1 + scenes - 1)

    pair = me + 1 - 2 * lax.rem(me, 2)
    half_strips = strips // 2

    def target(item):
        start = jnp.where(item < half_strips, me, pair)
        return lax.rem(start + 2 * lax.rem(item, half_strips), strips)

    def origin(item):
        start = jnp.where(item < half_strips, me, pair)
        return lax.rem(start + strips - 2 * lax.rem(item, half_strips), strips)

    def own_context(item):
        return pltpu.make_async_remote_copy(
            src_ref=context_hbm, dst_ref=context_all.at[me],
            send_sem=ctx_send.at[item], recv_sem=ctx_recv.at[me],
            device_id={"bev": target(item)}, device_id_type=MESH)

    def passed_context(item):
        source = origin(item)
        return pltpu.make_async_remote_copy(
            src_ref=context_all.at[source], dst_ref=context_all.at[source],
            send_sem=ctx_send.at[half_strips + item], recv_sem=ctx_recv.at[source],
            device_id={"bev": pair}, device_id_type=MESH)

    def context_arrived(item):
        source = origin(item)
        pltpu.make_async_remote_copy(
            src_ref=context_ref, dst_ref=context_all.at[source],
            send_sem=ctx_send.at[item], recv_sem=ctx_recv.at[source],
            device_id={"bev": source}, device_id_type=MESH).wait_recv()

    def slot_copy(item):
        to = target(item)
        return pltpu.make_async_remote_copy(
            src_ref=sent.at[to], dst_ref=got.at[me],
            send_sem=slot_send.at[item], recv_sem=slot_recv.at[me],
            device_id={"bev": to}, device_id_type=MESH)

    def slots_arrived(item):
        source = origin(item)
        pltpu.make_async_remote_copy(
            src_ref=sent.at[source], dst_ref=got.at[source],
            send_sem=slot_send.at[item], recv_sem=slot_recv.at[source],
            device_id={"bev": source}, device_id_type=MESH).wait_recv()

    @pl.loop(1, half_strips + 1)
    def _(item):
        own_context(item).start()

    loads[0].wait()
    logits = logits_ref[...]
    powers = jnp.exp(logits - jnp.max(logits, axis=0, keepdims=True))
    prob[...] = (powers / jnp.sum(powers, axis=0, keepdims=True)).astype(jnp.bfloat16)
    for copy in loads[1:]:
        copy.wait()
    context_all[me] = context_ref[...]
    row_ids[...] = lax.broadcasted_iota(jnp.int32, row_ids.shape, 0).astype(jnp.bfloat16)

    def hot_rows(count, ids):
        row = jnp.concatenate([row_ids[:count, :]] * (ids.shape[1] // LANES), axis=1)
        return jnp.where(row == ids.astype(jnp.bfloat16), jnp.bfloat16(1), jnp.bfloat16(0))

    points = point_ref[...]
    target_row = lax.broadcasted_iota(jnp.int32, points.shape, 0)
    counts = jnp.zeros_like(points)
    for d in range(strips):
        counts = jnp.where(target_row == d, count_ref[0, d], counts)
    live = lax.broadcasted_iota(jnp.int32, points.shape, 1) < counts
    pixels = points & (pix_block - 1)
    cells = jnp.where(live, cell_ref[...], strip_cells)
    point_ref[...] = pixels
    depth_table[...] = jnp.where(live, points >> log2(pix_block), depth_bins)
    code_table[...] = ((cells << log2(pix_block)) + pixels).astype(jnp.float32)
    depth_row = lax.broadcasted_iota(jnp.int32, (depth_bins, capacity), 0)

    def fill(to, slots, place):
        column = jnp.dot(prob[...], hot_rows(pix_block, point_ref[pl.ds(to, 1), :]),
                         preferred_element_type=jnp.float32)
        depth = depth_table[pl.ds(to, 1), :]
        weight = jnp.sum(jnp.where(depth_row == depth, column, 0.0), axis=0, keepdims=True)
        code = code_table[pl.ds(to, 1), :]
        for r in range(rows):
            slots[place, r:r + 1, :] = weight[:, r * LANES:(r + 1) * LANES]
            slots[place, rows + r:rows + r + 1, :] = code[:, r * LANES:(r + 1) * LANES]

    def fill_two(group):
        for item in (2 * group + 1, 2 * group + 2):
            fill(target(item), sent, target(item))
        for item in (2 * group + 1, 2 * group + 2):
            slot_copy(item).start()

    def pass_on(item):
        context_arrived(item)
        passed_context(item).start()

    fill_two(0)
    fill_two(1)

    @pl.loop(1, half_strips - 2)
    def _(item):
        pass_on(item)
        fill_two(item + 1)

    pass_on(half_strips - 2)
    fill(target(strips - 1), sent, target(strips - 1))
    slot_copy(strips - 1).start()
    fill(me, got, me)
    pass_on(half_strips - 1)

    def line(block):
        return jnp.concatenate([block[r:r + 1, :] for r in range(rows)], axis=1)

    def decode(source):
        code = got[source][rows:, :].astype(jnp.int32)
        return code & (pix_block - 1), code >> log2(pix_block)

    def scatter(half, cells, values):
        high = [((cell >> log2(quarter)) << log2(sub)) + (cell & (sub - 1)) - half * half_rows for cell in cells]
        low = [(cell >> log2(sub)) & (LOW - 1) for cell in cells]
        high = jnp.concatenate([line(block) for block in high], axis=1)
        low = jnp.concatenate([line(block) for block in low], axis=1).astype(jnp.bfloat16)
        values = jnp.concatenate(values, axis=1)
        low = jnp.broadcast_to(low, values.shape)
        spread = jnp.concatenate(
            [jnp.where(low == jnp.bfloat16(j), values, jnp.bfloat16(0)) for j in range(LOW)], axis=0)
        return lax.dot_general(
            spread, hot_rows(half_rows, high), (((1,), (1,)), ((), ())), preferred_element_type=jnp.float32)

    def form(source):
        pixel, cell = decode(source)
        features = jnp.dot(
            context_all[source], hot_rows(pix_block, line(pixel)), preferred_element_type=jnp.float32)
        values = (features * line(got[source][:rows, :])).astype(jnp.bfloat16)
        values_all[source] = values
        return cell, values

    near = scene // group
    far = lax.rem(near + 1, HALVES)

    def pool(*items):
        made = [form(origin(item)) for item in items]
        return scatter(far, [cell for cell, _ in made], [values for _, values in made])

    slots_arrived(1)
    total[...] = pool(0, 1)

    @pl.loop(1, half_strips // 2)
    def _(step):
        slots_arrived(2 * step)
        slots_arrived(2 * step + 1)
        total[...] += pool(2 * step, 2 * step + 1)

    @pl.loop(half_strips // 2, half_strips - 1)
    def _(step):
        for item in (2 * step, 2 * step + 1):
            slots_arrived(item)
            context_arrived(item)
        total[...] += pool(2 * step, 2 * step + 1)

    for item in (strips - 2, strips - 1):
        slots_arrived(item)
        context_arrived(item)
        total[...] += pool(item)

    def pack(half):
        for q in range(group):
            for j in range(LOW):
                parts[half * group + q, :, j * sub:(j + 1) * sub] = total[
                    j * channels:(j + 1) * channels, q * sub:(q + 1) * sub].astype(jnp.bfloat16)

    def place(source):
        return out_ref.at[pl.ds(pl.multiple_of(source * channels, 16), channels), :]

    def part_copy(to):
        return pltpu.make_async_remote_copy(
            src_ref=parts.at[to], dst_ref=place(scene),
            send_sem=part_send.at[to], recv_sem=part_recv.at[scene],
            device_id={"scene": to}, device_id_type=MESH)

    pack(far)
    for q in range(group):
        part_copy(far * group + q).start()

    def again(first):
        sources = [2 * first, 2 * first + 1]
        return scatter(near, [decode(source)[1] for source in sources], [values_all[source] for source in sources])

    total[...] = again(0)

    @pl.loop(1, half_strips)
    def _(step):
        total[...] += again(step)

    pack(near)
    others = [near * group + lax.rem(scene + o, group) for o in range(1, group)]
    for to in others:
        part_copy(to).start()
    out_ref[pl.ds(pl.multiple_of(scene * channels, 16), channels), :] = parts[scene]

    @pl.loop(1, strips)
    def _(step):
        slot_copy(step).wait_send()

    @pl.loop(1, half_strips + 1)
    def _(item):
        own_context(item).wait_send()

    @pl.loop(1, half_strips)
    def _(item):
        passed_context(item).wait_send()

    for to in [far * group + q for q in range(group)] + others:
        part_copy(to).wait_send()
        pltpu.make_async_remote_copy(
            src_ref=parts.at[to], dst_ref=place(to),
            send_sem=part_send.at[to], recv_sem=part_recv.at[to],
            device_id={"scene": to}, device_id_type=MESH).wait_recv()


def body(context, depth_logits, send_count, slot_point, slot_cell):
    strips = lax.axis_size("bev")
    scenes = lax.axis_size("scene")
    strip_cells = GRID * GRID // strips
    channels, pix_block = context.shape[1:]
    depth_bins = depth_logits.shape[1]
    capacity = slot_point.shape[3]
    quarter = strip_cells // scenes
    sub = quarter // LOW
    hbm = pl.BlockSpec(memory_space=pltpu.HBM)
    slots = (strips, 2 * capacity // LANES, LANES)
    pooled = pl.pallas_call(
        functools.partial(kernel, strips, scenes, strip_cells),
        out_shape=pltpu.VMEM((scenes * channels, quarter), jnp.bfloat16),
        in_specs=[hbm] * 5,
        out_specs=pl.BlockSpec(memory_space=pltpu.VMEM),
        scratch_shapes=[
            pltpu.VMEM((channels, pix_block), jnp.bfloat16),
            pltpu.VMEM((depth_bins, pix_block), jnp.float32),
            pltpu.SMEM((1, strips), jnp.int32),
            pltpu.VMEM((strips, capacity), jnp.int32),
            pltpu.VMEM((strips, capacity), jnp.int32),
            pltpu.VMEM((strips, capacity), jnp.int32),
            pltpu.VMEM((strips, capacity), jnp.float32),
            pltpu.VMEM((strips, channels, pix_block), jnp.bfloat16),
            pltpu.VMEM(slots, jnp.float32),
            pltpu.VMEM(slots, jnp.float32),
            pltpu.VMEM((depth_bins, pix_block), jnp.bfloat16),
            pltpu.VMEM((256, LANES), jnp.bfloat16),
            pltpu.VMEM((strips, channels, capacity), jnp.bfloat16),
            pltpu.VMEM((LOW * channels, scenes // HALVES * sub), jnp.float32),
            pltpu.VMEM((scenes, channels, quarter), jnp.bfloat16),
            pltpu.SemaphoreType.DMA((5,)),
            pltpu.SemaphoreType.DMA((strips,)),
            pltpu.SemaphoreType.DMA((strips,)),
            pltpu.SemaphoreType.DMA((strips,)),
            pltpu.SemaphoreType.DMA((strips,)),
            pltpu.SemaphoreType.DMA((scenes,)),
            pltpu.SemaphoreType.DMA((scenes,)),
        ],
        compiler_params=pltpu.CompilerParams(
            collective_id=0, has_side_effects=True, vmem_limit_bytes=63 * 1024 * 1024),
    )(context[0], depth_logits[0], send_count[0], slot_point[0, 0], slot_cell[0, 0])
    return jnp.transpose(pooled)


def solution(mesh):
    return jax.shard_map(
        body,
        mesh=mesh,
        in_specs=(
            P("scene", None, "bev"),
            P("scene", None, "bev"),
            P("scene", "bev", None),
            P("scene", "bev", None, None),
            P("scene", "bev", None, None),
        ),
        out_specs=P(("bev", "scene"), None),
        check_vma=False,
    )
```

```python
import functools

import jax
import jax.numpy as jnp
from jax import lax
from jax.experimental import pallas as pl
from jax.experimental.pallas import tpu as pltpu
from jax.sharding import PartitionSpec as P

GRID = 128
LANES = 128
LOW = 4
HALVES = 2
MESH = pl.DeviceIdType.MESH


def log2(size):
    assert size & (size - 1) == 0
    return size.bit_length() - 1


def kernel(strips, scenes, strip_cells, context_hbm, logits_hbm, count_hbm, point_hbm, cell_hbm,
           out_ref, context_ref, logits_ref, count_ref, point_ref, cell_ref, depth_table, code_table,
           context_all, sent, got, prob, row_ids, values_all, total, parts,
           load, ctx_send, ctx_recv, slot_send, slot_recv, part_send, part_recv):
    channels, pix_block = context_ref.shape
    depth_bins = logits_ref.shape[0]
    capacity = point_ref.shape[1]
    rows = capacity // LANES
    quarter = strip_cells // scenes
    sub = quarter // LOW
    group = scenes // HALVES
    half_rows = group * sub
    assert pix_block <= 256 and half_rows <= 256
    me = lax.axis_index("bev")
    scene = lax.axis_index("scene")

    loads = [
        pltpu.make_async_copy(src, dst, load.at[i])
        for i, (src, dst) in enumerate([
            (logits_hbm, logits_ref), (context_hbm, context_ref), (point_hbm, point_ref),
            (cell_hbm, cell_ref), (count_hbm, count_ref)])
    ]
    for copy in loads:
        copy.start()

    barrier = pltpu.get_barrier_semaphore()

    @pl.loop(1, strips)
    def _(step):
        pl.semaphore_signal(barrier, inc=1, device_id={"bev": lax.rem(me + step, strips)}, device_id_type=MESH)

    @pl.loop(1, scenes)
    def _(step):
        pl.semaphore_signal(barrier, inc=1, device_id={"scene": lax.rem(scene + step, scenes)}, device_id_type=MESH)

    pl.semaphore_wait(barrier, strips - 1 + scenes - 1)

    pair = me + 1 - 2 * lax.rem(me, 2)
    half_strips = strips // 2

    def target(item):
        start = jnp.where(item < half_strips, me, pair)
        return lax.rem(start + 2 * lax.rem(item, half_strips), strips)

    def origin(item):
        start = jnp.where(item < half_strips, me, pair)
        return lax.rem(start + strips - 2 * lax.rem(item, half_strips), strips)

    def own_context(item):
        return pltpu.make_async_remote_copy(
            src_ref=context_hbm, dst_ref=context_all.at[me],
            send_sem=ctx_send.at[item], recv_sem=ctx_recv.at[me],
            device_id={"bev": target(item)}, device_id_type=MESH)

    def passed_context(item):
        source = origin(item)
        return pltpu.make_async_remote_copy(
            src_ref=context_all.at[source], dst_ref=context_all.at[source],
            send_sem=ctx_send.at[half_strips + item], recv_sem=ctx_recv.at[source],
            device_id={"bev": pair}, device_id_type=MESH)

    def context_arrived(item):
        source = origin(item)
        pltpu.make_async_remote_copy(
            src_ref=context_ref, dst_ref=context_all.at[source],
            send_sem=ctx_send.at[item], recv_sem=ctx_recv.at[source],
            device_id={"bev": source}, device_id_type=MESH).wait_recv()

    def slot_copy(item):
        to = target(item)
        return pltpu.make_async_remote_copy(
            src_ref=sent.at[to], dst_ref=got.at[me],
            send_sem=slot_send.at[item], recv_sem=slot_recv.at[me],
            device_id={"bev": to}, device_id_type=MESH)

    def slots_arrived(item):
        source = origin(item)
        pltpu.make_async_remote_copy(
            src_ref=sent.at[source], dst_ref=got.at[source],
            send_sem=slot_send.at[item], recv_sem=slot_recv.at[source],
            device_id={"bev": source}, device_id_type=MESH).wait_recv()

    @pl.loop(1, half_strips + 1)
    def _(item):
        own_context(item).start()

    loads[0].wait()
    logits = logits_ref[...]
    powers = jnp.exp(logits - jnp.max(logits, axis=0, keepdims=True))
    prob[...] = (powers / jnp.sum(powers, axis=0, keepdims=True)).astype(jnp.bfloat16)
    for copy in loads[1:]:
        copy.wait()
    context_all[me] = context_ref[...]
    row_ids[...] = lax.broadcasted_iota(jnp.int32, row_ids.shape, 0).astype(jnp.bfloat16)

    def hot_rows(count, ids):
        row = jnp.concatenate([row_ids[:count, :]] * (ids.shape[1] // LANES), axis=1)
        return jnp.where(row == ids.astype(jnp.bfloat16), jnp.bfloat16(1), jnp.bfloat16(0))

    points = point_ref[...]
    target_row = lax.broadcasted_iota(jnp.int32, points.shape, 0)
    counts = jnp.zeros_like(points)
    for d in range(strips):
        counts = jnp.where(target_row == d, count_ref[0, d], counts)
    live = lax.broadcasted_iota(jnp.int32, points.shape, 1) < counts
    pixels = points & (pix_block - 1)
    cells = jnp.where(live, cell_ref[...], strip_cells)
    point_ref[...] = pixels
    depth_table[...] = jnp.where(live, points >> log2(pix_block), depth_bins)
    code_table[...] = ((cells << log2(pix_block)) + pixels).astype(jnp.float32)
    depth_row = lax.broadcasted_iota(jnp.int32, (depth_bins, capacity), 0)

    def fill(to, slots, place):
        column = jnp.dot(prob[...], hot_rows(pix_block, point_ref[pl.ds(to, 1), :]),
                         preferred_element_type=jnp.float32)
        depth = depth_table[pl.ds(to, 1), :]
        weight = jnp.sum(jnp.where(depth_row == depth, column, 0.0), axis=0, keepdims=True)
        code = code_table[pl.ds(to, 1), :]
        for r in range(rows):
            slots[place, r:r + 1, :] = weight[:, r * LANES:(r + 1) * LANES]
            slots[place, rows + r:rows + r + 1, :] = code[:, r * LANES:(r + 1) * LANES]

    def fill_two(group):
        for item in (2 * group + 1, 2 * group + 2):
            fill(target(item), sent, target(item))
        for item in (2 * group + 1, 2 * group + 2):
            slot_copy(item).start()

    def pass_on(item):
        context_arrived(item)
        passed_context(item).start()

    fill_two(0)
    fill_two(1)

    @pl.loop(1, half_strips - 2)
    def _(item):
        pass_on(item)
        fill_two(item + 1)

    pass_on(half_strips - 2)
    fill(target(strips - 1), sent, target(strips - 1))
    slot_copy(strips - 1).start()
    pass_on(half_strips - 1)
    fill(me, got, me)

    def line(block):
        return jnp.concatenate([block[r:r + 1, :] for r in range(rows)], axis=1)

    def decode(source):
        code = got[source][rows:, :].astype(jnp.int32)
        return code & (pix_block - 1), code >> log2(pix_block)

    def scatter(half, cells, values):
        high = [((cell >> log2(quarter)) << log2(sub)) + (cell & (sub - 1)) - half * half_rows for cell in cells]
        low = [(cell >> log2(sub)) & (LOW - 1) for cell in cells]
        high = jnp.concatenate([line(block) for block in high], axis=1)
        low = jnp.concatenate([line(block) for block in low], axis=1).astype(jnp.bfloat16)
        values = jnp.concatenate(values, axis=1)
        low = jnp.broadcast_to(low, values.shape)
        spread = jnp.concatenate(
            [jnp.where(low == jnp.bfloat16(j), values, jnp.bfloat16(0)) for j in range(LOW)], axis=0)
        return lax.dot_general(
            spread, hot_rows(half_rows, high), (((1,), (1,)), ((), ())), preferred_element_type=jnp.float32)

    def form(source):
        pixel, cell = decode(source)
        features = jnp.dot(
            context_all[source], hot_rows(pix_block, line(pixel)), preferred_element_type=jnp.float32)
        values = (features * line(got[source][:rows, :])).astype(jnp.bfloat16)
        values_all[source] = values
        return cell, values

    near = scene // group
    far = lax.rem(near + 1, HALVES)

    def form_two(first):
        made = [form(origin(item)) for item in (first, first + 1)]
        return scatter(far, [cell for cell, _ in made], [values for _, values in made])

    slots_arrived(1)
    total[...] = form_two(0)

    @pl.loop(1, half_strips // 2)
    def _(step):
        slots_arrived(2 * step)
        slots_arrived(2 * step + 1)
        total[...] += form_two(2 * step)

    @pl.loop(half_strips // 2, half_strips)
    def _(step):
        for item in (2 * step, 2 * step + 1):
            slots_arrived(item)
            context_arrived(item)
        total[...] += form_two(2 * step)

    def pack(half):
        for q in range(group):
            for j in range(LOW):
                parts[half * group + q, :, j * sub:(j + 1) * sub] = total[
                    j * channels:(j + 1) * channels, q * sub:(q + 1) * sub].astype(jnp.bfloat16)

    def place(source):
        return out_ref.at[pl.ds(pl.multiple_of(source * channels, 16), channels), :]

    def part_copy(to):
        return pltpu.make_async_remote_copy(
            src_ref=parts.at[to], dst_ref=place(scene),
            send_sem=part_send.at[to], recv_sem=part_recv.at[scene],
            device_id={"scene": to}, device_id_type=MESH)

    pack(far)
    for q in range(group):
        part_copy(far * group + q).start()

    def again(first):
        sources = [2 * first, 2 * first + 1]
        return scatter(near, [decode(source)[1] for source in sources], [values_all[source] for source in sources])

    total[...] = again(0)

    @pl.loop(1, half_strips)
    def _(step):
        total[...] += again(step)

    pack(near)
    others = [near * group + lax.rem(scene + o, group) for o in range(1, group)]
    for to in others:
        part_copy(to).start()
    out_ref[pl.ds(pl.multiple_of(scene * channels, 16), channels), :] = parts[scene]

    @pl.loop(1, strips)
    def _(step):
        slot_copy(step).wait_send()

    @pl.loop(1, half_strips + 1)
    def _(item):
        own_context(item).wait_send()

    @pl.loop(1, half_strips)
    def _(item):
        passed_context(item).wait_send()

    for to in [far * group + q for q in range(group)] + others:
        part_copy(to).wait_send()
        pltpu.make_async_remote_copy(
            src_ref=parts.at[to], dst_ref=place(to),
            send_sem=part_send.at[to], recv_sem=part_recv.at[to],
            device_id={"scene": to}, device_id_type=MESH).wait_recv()


def body(context, depth_logits, send_count, slot_point, slot_cell):
    strips = lax.axis_size("bev")
    scenes = lax.axis_size("scene")
    strip_cells = GRID * GRID // strips
    channels, pix_block = context.shape[1:]
    depth_bins = depth_logits.shape[1]
    capacity = slot_point.shape[3]
    quarter = strip_cells // scenes
    sub = quarter // LOW
    hbm = pl.BlockSpec(memory_space=pltpu.HBM)
    slots = (strips, 2 * capacity // LANES, LANES)
    pooled = pl.pallas_call(
        functools.partial(kernel, strips, scenes, strip_cells),
        out_shape=pltpu.VMEM((scenes * channels, quarter), jnp.bfloat16),
        in_specs=[hbm] * 5,
        out_specs=pl.BlockSpec(memory_space=pltpu.VMEM),
        scratch_shapes=[
            pltpu.VMEM((channels, pix_block), jnp.bfloat16),
            pltpu.VMEM((depth_bins, pix_block), jnp.float32),
            pltpu.SMEM((1, strips), jnp.int32),
            pltpu.VMEM((strips, capacity), jnp.int32),
            pltpu.VMEM((strips, capacity), jnp.int32),
            pltpu.VMEM((strips, capacity), jnp.int32),
            pltpu.VMEM((strips, capacity), jnp.float32),
            pltpu.VMEM((strips, channels, pix_block), jnp.bfloat16),
            pltpu.VMEM(slots, jnp.float32),
            pltpu.VMEM(slots, jnp.float32),
            pltpu.VMEM((depth_bins, pix_block), jnp.bfloat16),
            pltpu.VMEM((256, LANES), jnp.bfloat16),
            pltpu.VMEM((strips, channels, capacity), jnp.bfloat16),
            pltpu.VMEM((LOW * channels, scenes // HALVES * sub), jnp.float32),
            pltpu.VMEM((scenes, channels, quarter), jnp.bfloat16),
            pltpu.SemaphoreType.DMA((5,)),
            pltpu.SemaphoreType.DMA((strips,)),
            pltpu.SemaphoreType.DMA((strips,)),
            pltpu.SemaphoreType.DMA((strips,)),
            pltpu.SemaphoreType.DMA((strips,)),
            pltpu.SemaphoreType.DMA((scenes,)),
            pltpu.SemaphoreType.DMA((scenes,)),
        ],
        compiler_params=pltpu.CompilerParams(
            collective_id=0, has_side_effects=True, vmem_limit_bytes=63 * 1024 * 1024),
    )(context[0], depth_logits[0], send_count[0], slot_point[0, 0], slot_cell[0, 0])
    return jnp.transpose(pooled)


def solution(mesh):
    return jax.shard_map(
        body,
        mesh=mesh,
        in_specs=(
            P("scene", None, "bev"),
            P("scene", None, "bev"),
            P("scene", "bev", None),
            P("scene", "bev", None, None),
            P("scene", "bev", None, None),
        ),
        out_specs=P(("bev", "scene"), None),
        check_vma=False,
    )
```
